128 devices in a mesh: vid: 16 (over y_hi, z, core), tm: 8 (over y_lo, x).
Axes of the slice: x: 4, y: 4 (y_hi: 2, y_lo: 2; y = y_hi * 2 + y_lo), z: 4, core: 2. Of those that a mesh axis runs over, the one named last changes fastest.
Arguments:
- tokens: bfloat16 [16, 1024, 16, 1024], P('vid', 'tm'), may hold values from -6 to 6
- norm_gain: float32 [1024], replicated, may hold values from 0.1 to 1.9
- w_qkv: bfloat16 [1024, 3072], replicated, may hold values from -0.1875 to 0.1875
- w_out: bfloat16 [1024, 1024], replicated, may hold values from -0.1875 to 0.1875
- w_proj: bfloat16 [1024, 2048], replicated, may hold values from -0.1875 to 0.1875
- offsets: int32 [16, 1024], P('vid', 'tm'), may hold values from -8 to 8, as said below
- negatives: int32 [16, 1024, 8], P(None, 'tm'), may hold values from 0 to 15, as said below
- valid: int32 [16], replicated, may hold values from 528 to 1024
Outputs:
- embeddings: bfloat16 [16, 1024, 2048], P('vid', 'tm')
- losses: float32 [16, 1024], P('vid', 'tm')
The draws below stay inside these ranges and needn't reach their ends.
Inputs may be any that keep to these rules, and one draw needn't show every extreme that they name: `negatives`: a negative id never equals the anchor's own video. `offsets`: an offset is never 0.
All inputs are finite; a program needn't handle non-finite values.
Results may differ from the reference program's by a relative error of at most 0.015.
Values may be sent and summed in bfloat16 or wider, within the bound.
A program may use at most 128 MiB of HBM per device.

```python
import jax
import jax.numpy as jnp
from jax import lax

D = 1024
HEADS = 16
HEAD = 64
E = 2048
PATCH = 16
WINDOW = 16
REACH = 8
NEG = 8
FRAMES = 1024
VIDEOS = 16


def draw_negatives(key, part):
    key = jax.random.fold_in(key, 7)
    jumps = jax.random.randint(key, (VIDEOS, FRAMES, NEG), 1, VIDEOS)
    own = jnp.arange(VIDEOS, dtype=jnp.int32)[:, None, None]
    return ((own + jumps) % VIDEOS).astype(jnp.int32)


def draw_offsets(key, part):
    key = jax.random.fold_in(key, 11)
    key_size, key_sign = jax.random.split(key)
    magnitude = jax.random.randint(key_size, (VIDEOS, FRAMES), 1, REACH + 1)
    direction = jax.random.randint(key_sign, (VIDEOS, FRAMES), 0, 2) * 2 - 1
    return (magnitude * direction).astype(jnp.int32)


def with_ends(array, stream_key, least, largest):
    index_at = [jax.random.randint(jax.random.fold_in(stream_key, axis), (), 0, length) for axis, length in enumerate(array.shape)]
    main_axis = array.shape.index(max(array.shape))
    neighbour = index_at[:main_axis] + [(index_at[main_axis] + 1) % array.shape[main_axis]] + index_at[main_axis + 1:]
    return array.at[tuple(index_at)].set(least).at[tuple(neighbour)].set(largest)


def block_scale(own_key, dims, pieces, smallest, high):
    def one(position, shards_of):
        heights = jax.random.uniform(jax.random.fold_in(jax.random.fold_in(own_key, 6), position), (shards_of,), jnp.float32, smallest / len(pieces), high / len(pieces))
        return jnp.repeat(jnp.exp(heights), dims[position] // shards_of).reshape((-1,) + (1,) * (len(dims) - position - 1))

    loudness = one(*pieces[0])
    for cut in pieces[1:]:
        loudness = loudness * one(*cut)
    return loudness


def scatter_about(key, extent, spread, reach, pieces=(), held_as=jnp.bfloat16):
    entries = spread * jax.random.normal(key, extent, jnp.float32)
    if pieces:
        entries = entries * block_scale(key, extent, pieces, -0.22, 0.18)
    return jnp.clip(entries, -reach, reach).astype(held_as)


def setup_inputs(seed: int = 0) -> dict:
    arg_keys = jax.random.split(jax.random.key(seed), 9)
    return {
        "tokens": scatter_about(arg_keys[0], (VIDEOS, FRAMES, PATCH, D), 1.0, 6.0, ((0, 16), (1, 8))),
        "norm_gain": jnp.clip(1.0 + 0.18 * jax.random.normal(arg_keys[1], (D,), jnp.float32), 0.1, 1.9),
        "w_qkv": scatter_about(arg_keys[2], (D, 3 * D), D ** -0.5, 0.1875),
        "w_out": scatter_about(arg_keys[3], (D, D), D ** -0.5, 0.1875),
        "w_proj": scatter_about(arg_keys[4], (D, E), D ** -0.5, 0.1875),
        "offsets": draw_offsets(jax.random.fold_in(arg_keys[8], 71), 0),
        "negatives": draw_negatives(jax.random.fold_in(arg_keys[8], 71), 0),
        "valid": with_ends(jax.random.randint(arg_keys[7], (VIDEOS,), FRAMES // 2 + 2 * REACH, FRAMES + 1), jax.random.fold_in(arg_keys[7], 1), FRAMES // 2 + 2 * REACH, FRAMES).astype(jnp.int32),
    }


def one_video(item, norm_gain, w_qkv, w_out, w_proj):
    video, length = item
    xf = video.astype(jnp.float32)
    scale = lax.rsqrt(lax.optimization_barrier(jnp.mean(xf * xf, axis=-1, keepdims=True)) + 1e-05)
    normed = (xf * scale * norm_gain).astype(jnp.bfloat16)
    flat = normed.reshape(FRAMES * PATCH, D)
    qkv = jnp.dot(flat, w_qkv, preferred_element_type=jnp.float32).astype(jnp.bfloat16)
    qkv = qkv.reshape(FRAMES, PATCH, 3, HEADS, HEAD).astype(jnp.float32)
    query, keys, values = (qkv[:, :, 0], qkv[:, :, 1], qkv[:, :, 2])
    scores = jnp.einsum('fphc,gphc->phfg', query, keys) / jnp.sqrt(jnp.float32(HEAD))
    rows = jnp.arange(FRAMES)[:, None]
    cols = jnp.arange(FRAMES)[None, :]
    allowed = (jnp.abs(rows - cols) <= WINDOW) & ((cols < length) | (cols == rows))
    scores = jnp.where(allowed, scores, -1e+30)
    probs = jax.nn.softmax(scores, axis=-1).astype(jnp.bfloat16).astype(jnp.float32)
    attended_tokens = jnp.einsum('phfg,gphc->fphc', probs, values).astype(jnp.bfloat16)
    attended_tokens = attended_tokens.reshape(FRAMES * PATCH, D)
    hidden = xf + jnp.dot(attended_tokens, w_out, preferred_element_type=jnp.float32).reshape(FRAMES, PATCH, D)
    pooled = lax.optimization_barrier(jnp.mean(hidden, axis=1)).astype(jnp.bfloat16)
    return jnp.dot(pooled, w_proj, preferred_element_type=jnp.float32).astype(jnp.bfloat16)

def reference(tokens, norm_gain, w_qkv, w_out, w_proj, offsets, negatives, valid):
    embeddings = lax.map(lambda item: one_video(item, norm_gain, w_qkv, w_out, w_proj), (tokens, valid))
    frame_ids = jnp.arange(FRAMES).astype(jnp.int32)
    ahead = frame_ids[None, :] + offsets
    inside = (ahead >= 0) & (ahead < valid[:, None])
    positive = jnp.where(inside, ahead, frame_ids[None, :] - offsets).astype(jnp.int32)
    zf = embeddings.astype(jnp.float32)
    zpos = jnp.take_along_axis(zf, positive[:, :, None], axis=1)
    factor = 8.0 / jnp.sqrt(jnp.float32(E))
    pos = lax.optimization_barrier(jnp.sum(zf * zpos, axis=-1)) * factor
    zneg = zf[negatives, frame_ids[None, :, None]]
    negative_sample = jnp.einsum('nte,ntke->ntk', zf, zneg) * factor
    neg_ok = frame_ids[None, :, None] < valid[negatives]
    negative_sample = jnp.where(neg_ok, negative_sample, -1e+30)
    every = jnp.concatenate([pos[:, :, None], negative_sample], axis=-1)
    top = lax.optimization_barrier(jnp.max(every, axis=-1))
    lse = top + jnp.log(lax.optimization_barrier(jnp.sum(jnp.exp(every - top[:, :, None]), axis=-1)))
    losses = jnp.where(frame_ids[None, :] < valid[:, None], lse - pos, 0.0)
    return (embeddings, losses)
```

```python
import functools
import math

import jax
import jax.numpy as jnp
from jax import lax
from jax.experimental import pallas as pl
from jax.experimental.pallas import tpu as pltpu
from jax.sharding import PartitionSpec as P

MESH = pl.DeviceIdType.MESH
BF, F32, I32 = jnp.bfloat16, jnp.float32, jnp.int32
D = 1024
E = 2048
PATCH = 16
WINDOW = 16
REACH = 8
COUNT = 128
VIDS = 16
TMS = 8
NEG = 8
PART = COUNT // VIDS
HALF = D // 2


def nn(a, b):
    return lax.dot_general(a, b, (((1,), (0,)), ((), ())), preferred_element_type=F32)


def nt(a, b):
    return lax.dot_general(a, b, (((1,), (1,)), ((), ())), preferred_element_type=F32)


def iota(shape, dim):
    return lax.broadcasted_iota(I32, shape, dim)


def kernel(
    valid, tokens, gain, w_qkv, w_out, w_proj, offsets, negatives,
    emb_out, loss_out,
    raw, halo, wq, wk, wv, wo, wp, negs, wqvt, xn, xh, keys, keys_h, qt, vt, vt_h,
    bias, tokmean, acc, pack, got, near, own_e, count, lse_out, lse_in,
    tok_sem, w_sem, out_sem, halo_send, halo_recv, a_send, a_recv, n_send, n_recv, b_send, b_recv,
):
    vid = lax.axis_index("vid")
    tm = lax.axis_index("tm")
    left = lax.rem(tm + TMS - 1, TMS)
    right = lax.rem(tm + 1, TMS)
    peers = [lax.rem(vid + k, VIDS) for k in range(VIDS)]
    first = tm * COUNT
    length = valid[vid]

    tok_copies = [
        pltpu.make_async_copy(tokens.at[pl.ds(256 * b, 256)], raw.at[b], tok_sem.at[b])
        for b in range(8)
    ]
    w_copies = [
        pltpu.make_async_copy(src, dst, w_sem.at[i])
        for i, (src, dst) in enumerate(
            [
                (w_qkv.at[:, pl.ds(0, D)], wq),
                (w_qkv.at[:, pl.ds(2 * D, D)], wv),
                (w_qkv.at[:, pl.ds(D, D)], wk),
                (w_out, wo),
                (w_proj, wp),
                (negatives.at[:, pl.ds(pl.multiple_of(PART * vid, PART), PART), :], negs),
            ]
        )
    ]
    barrier = pltpu.get_barrier_semaphore()
    for peer in peers[1:]:
        pl.semaphore_signal(barrier, inc=1, device_id={"vid": peer}, device_id_type=MESH)
    for peer in (left, right):
        pl.semaphore_signal(barrier, inc=1, device_id={"tm": peer}, device_id_type=MESH)
    w_copies[0].start()
    tok_copies[0].start()
    w_copies[1].start()
    for copy in tok_copies[1:]:
        copy.start()
    for copy in w_copies[2:]:
        copy.start()
    pl.semaphore_wait(barrier, VIDS + 1)

    halo_copies = [
        pltpu.make_async_remote_copy(
            src_ref=tokens.at[pl.ds(256 * 7, 256)], dst_ref=halo.at[0],
            send_sem=halo_send.at[0], recv_sem=halo_recv.at[0],
            device_id={"tm": right}, device_id_type=MESH,
        ),
        pltpu.make_async_remote_copy(
            src_ref=tokens.at[pl.ds(0, 256)], dst_ref=halo.at[1],
            send_sem=halo_send.at[1], recv_sem=halo_recv.at[1],
            device_id={"tm": left}, device_id_type=MESH,
        ),
    ]
    for copy in halo_copies:
        copy.start()

    r0, r1 = iota((256, 256), 0), iota((256, 256), 1)
    perm = (r1 == (r0 % 16) * 16 + r0 // 16).astype(F32).astype(BF)
    eye = (r0 == r1).astype(F32).astype(BF)

    g0, f0 = iota((160, COUNT), 0), iota((160, COUNT), 1)
    frame = jnp.where(g0 < COUNT, g0, jnp.where(g0 < COUNT + WINDOW, g0 - COUNT - WINDOW, g0 - WINDOW))
    glob = frame + first
    ok = (jnp.abs(frame - f0) <= WINDOW) & (glob >= 0) & (glob < TMS * COUNT)
    ok = ok & ((glob < length) | (frame == f0))
    bias[...] = jnp.where(ok, 0.0, -1e30)

    w_copies[0].wait()

    def flip(src, base, scale):
        def body(i, carry):
            a = pl.multiple_of((i // 4) * 256, 256)
            b = pl.multiple_of((i % 4) * 256, 256)
            block = nt(eye, src[pl.ds(b, 256), pl.ds(a, 256)])
            wqvt[pl.ds(base + a, 256), pl.ds(b, 256)] = block.astype(BF)
            return carry
        lax.fori_loop(0, 16, body, 0)

    flip(wq, 0, 1.0)
    w_copies[1].wait()
    flip(wv, D, 1.0)

    def normed(block):
        x = nn(perm, block)
        ms = jnp.mean(x * x, axis=1, keepdims=True)
        return x, (x * lax.rsqrt(ms + 1e-5) * gain[...]).astype(BF)

    for b in range(8):
        tok_copies[b].wait()

    def norm_block(b, carry):
        x, y = normed(raw[b])
        rows = pl.ds(pl.multiple_of(16 * b, 16), 16)
        xn[:, rows, :] = y.reshape(PATCH, 16, D)
        tokmean[rows, :] = jnp.sum(x.reshape(PATCH, 16, D), axis=0) * (1.0 / PATCH)
        return carry

    lax.fori_loop(0, 8, norm_block, 0)

    w_copies[2].wait()
    scale = math.log2(math.e) / 8.0

    def project(i, carry):
        x2 = xn[pl.ds(2 * i, 2)].reshape(256, D)
        keys[pl.ds(2 * i, 2)] = nn(x2, wk[...]).astype(BF).reshape(2, COUNT, D)
        for c in range(2):
            r = nt(wqvt[512 * c:512 * c + 512], x2) * scale
            qt[2 * i, pl.ds(512 * c, 512), :] = r[:, :COUNT].astype(BF)
            qt[2 * i + 1, pl.ds(512 * c, 512), :] = r[:, COUNT:].astype(BF)
        for c in range(2):
            r = nt(wqvt[D + 512 * c:D + 512 * c + 512], x2)
            vt[2 * i, pl.ds(512 * c, 512), :] = r[:, :COUNT].astype(BF)
            vt[2 * i + 1, pl.ds(512 * c, 512), :] = r[:, COUNT:].astype(BF)
        return carry

    lax.fori_loop(0, 8, project, 0)

    for s in range(2):
        halo_copies[s].wait_recv()
        _, y = normed(halo[s])
        xh[:, 16 * s:16 * s + 16, :] = y.reshape(PATCH, 16, D)
    flat = xh[...].reshape(2 * 256, D)
    keys_h[...] = nn(flat, wk[...]).astype(BF).reshape(PATCH, 32, D)

    def project_h(c, carry):
        rows = pl.ds(pl.multiple_of(256 * c, 256), 256)
        r = nt(wqvt[pl.ds(pl.multiple_of(D + 256 * c, 256), 256)], xh[...].reshape(512, D)).astype(BF)
        for g in range(4):
            vt_h[g, rows, :] = r[:, 128 * g:128 * g + 128]
        return carry

    lax.fori_loop(0, 4, project_h, 0)

    acc[...] = jnp.zeros_like(acc)
    ones = jnp.ones((16, 256), BF)

    def attend(it, carry):
        g = it // 8
        cols = pl.ds(pl.multiple_of((it % 8) * 128, 128), 128)
        sums = [jnp.zeros((64, COUNT), F32)] * 2
        zq = jnp.zeros((64, COUNT), BF)
        zh = jnp.zeros((32, COUNT), BF)
        for q in range(4):
            p = 4 * g + q
            k = jnp.concatenate([keys[p, :, cols], keys_h[p, :, cols]], axis=0)
            ql = qt[p, cols, :]
            qbd = jnp.concatenate(
                [jnp.concatenate([ql[:64], zq], axis=1), jnp.concatenate([zq, ql[64:]], axis=1)], axis=0
            )
            st = nn(k, qbd)
            v = jnp.concatenate([vt[p, cols, :], vt_h[g, cols, :]], axis=1)
            for h in range(2):
                s = st[:, 128 * h:128 * h + 128] + bias[...]
                e = jnp.exp2(s - jnp.max(s, axis=0, keepdims=True)).astype(BF)
                e = jnp.concatenate([e[:COUNT]] + [zh] * q + [e[COUNT:]] + [zh] * (3 - q), axis=0)
                o = nn(jnp.concatenate([v[64 * h:64 * h + 64], ones], axis=0), e)
                sums[h] = sums[h] + o[:64] * (1.0 / o[64:65])
        acc[cols, :] += jnp.concatenate(sums, axis=0)
        return carry

    lax.fori_loop(0, 32, attend, 0)

    w_copies[3].wait()
    att = jnp.transpose(acc[...] * (1.0 / PATCH)).astype(BF)
    pooled = tokmean[...] + nn(att, wo[...])
    blocks = pooled.reshape(VIDS, PART, D)
    pack[...] = jnp.concatenate([blocks[:, :, :HALF], blocks[:, :, HALF:]], axis=1).astype(BF)

    pooled_copies = [
        pltpu.make_async_remote_copy(
            src_ref=pack.at[peers[k]], dst_ref=got.at[vid],
            send_sem=a_send.at[k], recv_sem=a_recv.at[k],
            device_id={"vid": peers[k]}, device_id_type=MESH,
        )
        for k in range(1, VIDS)
    ]
    near_copies = [
        pltpu.make_async_remote_copy(
            src_ref=pack.at[VIDS - 1], dst_ref=near.at[0],
            send_sem=n_send.at[0], recv_sem=n_recv.at[0],
            device_id={"tm": right}, device_id_type=MESH,
        ),
        pltpu.make_async_remote_copy(
            src_ref=pack.at[0], dst_ref=near.at[1],
            send_sem=n_send.at[1], recv_sem=n_recv.at[1],
            device_id={"tm": left}, device_id_type=MESH,
        ),
    ]
    for copy in pooled_copies + near_copies:
        copy.start()
    got[vid] = pack[vid]

    w_copies[4].wait()
    own_e[...] = nn(pooled.astype(BF), wp[...]).astype(BF)
    out_copy = pltpu.make_async_copy(own_e, emb_out, out_sem)
    out_copy.start()

    w_copies[5].wait()
    lane = iota((COUNT, COUNT), 1)
    row = iota((COUNT, COUNT), 0)
    ids = negs[...].reshape(COUNT, NEG)
    times = jnp.zeros((COUNT, COUNT), F32)
    for k in range(NEG):
        times += (ids[:, k:k + 1] * PART + row % PART == lane).astype(F32)
    count[...] = times

    e = own_e[...]
    near_own = nt(e, e)

    for copy in near_copies + pooled_copies:
        copy.wait_recv()
    seen = jnp.concatenate([got[...], near[...]], axis=0).astype(F32)
    seen = jnp.concatenate([seen[:, :PART], seen[:, PART:]], axis=2)
    seen = seen.reshape((VIDS + 2) * PART, D).astype(BF)
    all_e = nn(seen, wp[...]).astype(BF)
    factor = 8.0 / math.sqrt(E)
    gram = nt(all_e[:COUNT], all_e[:COUNT]) * factor

    frame_here = first + PART * vid + lane % PART
    other = jnp.zeros((COUNT, COUNT), I32)
    for m in range(VIDS):
        other = jnp.where(lane // PART == m, valid[m], other)
    times = count[...]
    neg = jnp.where(frame_here < other, gram, -1e30)
    top = jnp.max(jnp.where(times > 0, neg, -3e38), axis=1, keepdims=True)
    some = jnp.sum(jnp.where(times > 0, times * jnp.exp(jnp.minimum(neg - top, 0.0)), 0.0), axis=1, keepdims=True)
    lse = top + jnp.log(some)
    lse_out[...] = jnp.broadcast_to(lse, (COUNT, 128)).reshape(VIDS, PART, 128)

    back_copies = [
        pltpu.make_async_remote_copy(
            src_ref=lse_out.at[peers[k]], dst_ref=lse_in.at[vid],
            send_sem=b_send.at[k], recv_sem=b_recv.at[k],
            device_id={"vid": peers[k]}, device_id_type=MESH,
        )
        for k in range(1, VIDS)
    ]
    for copy in back_copies:
        copy.start()
    lse_in[vid] = lse_out[vid]

    near_e = nt(all_e[COUNT:], e)
    scores = jnp.concatenate([near_e[:REACH], near_own, near_e[REACH:]], axis=0)
    off = offsets[...]
    here = first + iota((1, COUNT), 1)
    ahead = here + off
    inside = (ahead >= 0) & (ahead < length)
    slot = jnp.where(inside, ahead, here - off) - first + REACH
    pick = iota((COUNT + 2 * REACH, COUNT), 0) == slot
    pos = jnp.sum(jnp.where(pick, scores, 0.0), axis=0, keepdims=True) * factor

    for copy in back_copies:
        copy.wait_recv()
    back = lse_in[...].reshape(COUNT, 128)
    lse_neg = jnp.sum(jnp.where(row == lane, back, 0.0), axis=0, keepdims=True)
    peak = jnp.maximum(pos, lse_neg)
    total = peak + jnp.log(jnp.exp(pos - peak) + jnp.exp(lse_neg - peak))
    loss_out[...] = jnp.where(here < length, total - pos, 0.0)

    for copy in halo_copies + pooled_copies + near_copies + back_copies:
        copy.wait_send()
    out_copy.wait()


def local(tokens, norm_gain, w_qkv, w_out, w_proj, offsets, negatives, valid):
    anywhere = pl.BlockSpec(memory_space=pl.ANY)
    vmem = pl.BlockSpec(memory_space=pltpu.VMEM)
    dma = pltpu.SemaphoreType.DMA
    emb, losses = pl.pallas_call(
        kernel,
        out_shape=(
            jax.ShapeDtypeStruct((COUNT, E), BF),
            jax.ShapeDtypeStruct((1, COUNT), F32),
        ),
        in_specs=[
            pl.BlockSpec(memory_space=pltpu.SMEM), anywhere, vmem, anywhere, anywhere, anywhere, vmem, anywhere,
        ],
        out_specs=(anywhere, vmem),
        scratch_shapes=[
            pltpu.VMEM((8, 256, D), BF),
            pltpu.VMEM((2, 256, D), BF),
            pltpu.VMEM((D, D), BF),
            pltpu.VMEM((D, D), BF),
            pltpu.VMEM((D, D), BF),
            pltpu.VMEM((D, D), BF),
            pltpu.VMEM((D, E), BF),
            pltpu.VMEM((VIDS, PART, NEG), I32),
            pltpu.VMEM((2 * D, D), BF),
            pltpu.VMEM((PATCH, COUNT, D), BF),
            pltpu.VMEM((PATCH, 32, D), BF),
            pltpu.VMEM((PATCH, COUNT, D), BF),
            pltpu.VMEM((PATCH, 32, D), BF),
            pltpu.VMEM((PATCH, D, COUNT), BF),
            pltpu.VMEM((PATCH, D, COUNT), BF),
            pltpu.VMEM((4, D, 128), BF),
            pltpu.VMEM((160, COUNT), F32),
            pltpu.VMEM((COUNT, D), F32),
            pltpu.VMEM((D, COUNT), F32),
            pltpu.VMEM((VIDS, 16, HALF), BF),
            pltpu.VMEM((VIDS, 16, HALF), BF),
            pltpu.VMEM((2, 16, HALF), BF),
            pltpu.VMEM((COUNT, E), BF),
            pltpu.VMEM((COUNT, COUNT), F32),
            pltpu.VMEM((VIDS, PART, 128), F32),
            pltpu.VMEM((VIDS, PART, 128), F32),
            dma((8,)), dma((6,)), dma, dma((2,)), dma((2,)), dma((VIDS,)), dma((VIDS,)),
            dma((2,)), dma((2,)), dma((VIDS,)), dma((VIDS,)),
        ],
        compiler_params=pltpu.CompilerParams(
            collective_id=0, has_side_effects=True, vmem_limit_bytes=60 * 1024 * 1024
        ),
    )(
        valid,
        tokens.reshape(COUNT * PATCH, D),
        norm_gain.reshape(1, D),
        w_qkv,
        w_out,
        w_proj,
        offsets,
        negatives,
    )
    return emb.reshape(1, COUNT, E), losses


def solution(mesh):
    placed = (
        P("vid", "tm", None, None),
        P(),
        P(),
        P(),
        P(),
        P("vid", "tm"),
        P(None, "tm", None),
        P(),
    )
    return jax.shard_map(
        local,
        mesh=mesh,
        in_specs=placed,
        out_specs=(P("vid", "tm", None), P("vid", "tm")),
        check_vma=False,
    )
```

```python
import functools
import math

import jax
import jax.numpy as jnp
from jax import lax
from jax.experimental import pallas as pl
from jax.experimental.pallas import tpu as pltpu
from jax.sharding import PartitionSpec as P

MESH = pl.DeviceIdType.MESH
BF, F32, I32 = jnp.bfloat16, jnp.float32, jnp.int32
D = 1024
E = 2048
PATCH = 16
WINDOW = 16
REACH = 8
COUNT = 128
VIDS = 16
TMS = 8
NEG = 8
PART = COUNT // VIDS
HALF = D // 2


def nn(a, b):
    return lax.dot_general(a, b, (((1,), (0,)), ((), ())), preferred_element_type=F32)


def nt(a, b):
    return lax.dot_general(a, b, (((1,), (1,)), ((), ())), preferred_element_type=F32)


def iota(shape, dim):
    return lax.broadcasted_iota(I32, shape, dim)


def kernel(
    valid, tokens, gain, w_qkv, w_out, w_proj, offsets, negatives,
    emb_out, loss_out,
    raw, halo, wq, wk, wv, wo, negs, negt, wqvt, xn, keys, qbd, vt, y0, y1,
    bias, st0, st1, pr0, pr1, tokmean, acc, pack, got, near, own_e, count, lse_out, lse_in,
    tok_sem, w_sem, out_sem, halo_send, halo_recv, a_send, a_recv, n_send, n_recv, b_send, b_recv,
):
    vid = lax.axis_index("vid")
    tm = lax.axis_index("tm")
    left = lax.rem(tm + TMS - 1, TMS)
    right = lax.rem(tm + 1, TMS)
    peers = [lax.rem(vid + k, VIDS) for k in range(VIDS)]
    first = tm * COUNT
    length = valid[vid]

    tok_copies = [
        pltpu.make_async_copy(tokens.at[pl.ds(256 * b, 256)], raw.at[b], tok_sem.at[b])
        for b in range(8)
    ]
    w_copies = [
        pltpu.make_async_copy(src, dst, w_sem.at[i])
        for i, (src, dst) in enumerate(
            [
                (w_qkv.at[:, pl.ds(0, D)], wq),
                (w_qkv.at[:, pl.ds(2 * D, D)], wv),
                (w_qkv.at[:, pl.ds(D, D)], wk),
                (w_out, wo),
                (negatives, negs),
                (w_proj.at[:, pl.ds(0, D)], wq),
                (w_proj.at[:, pl.ds(D, D)], wv),
            ]
        )
    ]
    barrier = pltpu.get_barrier_semaphore()
    for peer in peers[1:]:
        pl.semaphore_signal(barrier, inc=1, device_id={"vid": peer}, device_id_type=MESH)
    for peer in (left, right):
        pl.semaphore_signal(barrier, inc=1, device_id={"tm": peer}, device_id_type=MESH)
    w_copies[0].start()
    tok_copies[0].start()
    w_copies[1].start()
    for copy in tok_copies[1:]:
        copy.start()
    for copy in w_copies[2:5]:
        copy.start()
    pl.semaphore_wait(barrier, VIDS + 1)

    halo_copies = [
        pltpu.make_async_remote_copy(
            src_ref=tokens.at[pl.ds(256 * 7, 256)], dst_ref=halo.at[0],
            send_sem=halo_send.at[0], recv_sem=halo_recv.at[0],
            device_id={"tm": right}, device_id_type=MESH,
        ),
        pltpu.make_async_remote_copy(
            src_ref=tokens.at[pl.ds(0, 256)], dst_ref=halo.at[1],
            send_sem=halo_send.at[1], recv_sem=halo_recv.at[1],
            device_id={"tm": left}, device_id_type=MESH,
        ),
    ]
    for copy in halo_copies:
        copy.start()

    r0, r1 = iota((256, 256), 0), iota((256, 256), 1)
    perm = (r1 == (r0 % 16) * 16 + r0 // 16).astype(F32).astype(BF)
    eye = (r0 == r1).astype(F32).astype(BF)
    avg = jnp.where(iota((16, 256), 0) == iota((16, 256), 1) // 16, 1.0 / PATCH, 0.0).astype(BF)

    g0, f0 = iota((64, 128), 0), iota((64, 128), 1) % 32
    for b in range(4):
        frame = g0 + (32 * b - WINDOW)
        query = f0 + 32 * b
        glob = frame + first
        ok = (jnp.abs(frame - query) <= WINDOW) & (glob >= 0) & (glob < TMS * COUNT)
        ok = ok & ((glob < length) | (frame == query))
        bias[b] = jnp.where(ok, 0.0, -1e30)
    lane_block = iota((64, 128), 1) // 32

    w_copies[4].wait()
    lane = iota((COUNT, COUNT), 1)
    row = iota((COUNT, COUNT), 0)
    negt[...] = jnp.transpose(negs[...].reshape(VIDS * NEG, COUNT).astype(F32))
    ids = negt[pl.ds(pl.multiple_of(PART * vid, PART), PART), :]
    ids = jnp.concatenate([ids] * VIDS, axis=0)
    times = jnp.zeros((COUNT, COUNT), F32)
    for k in range(NEG):
        one = jnp.sum(jnp.where(lane == row // PART * NEG + k, ids, 0.0), axis=1, keepdims=True)
        times += (one * PART + (row % PART).astype(F32) == lane.astype(F32)).astype(F32)
    count[...] = times

    w_copies[0].wait()

    def flip(src, base):
        def body(i, carry):
            a = pl.multiple_of(i * 256, 256)
            for c in range(4):
                block = nt(eye, src[256 * c:256 * c + 256, pl.ds(a, 256)])
                wqvt[pl.ds(base + a, 256), 256 * c:256 * c + 256] = block.astype(BF)
            return carry
        lax.fori_loop(0, 4, body, 0)

    flip(wq, 0)
    w_copies[1].wait()
    flip(wv, D)
    w_copies[5].start()
    w_copies[6].start()

    def normed(block, rows, out):
        x = nn(perm, block)
        ms = jnp.mean(x * x, axis=1, keepdims=True)
        y = (x * lax.rsqrt(ms + 1e-5) * gain[...]).astype(BF)
        out[...] = y
        xn[:, rows, :] = y.reshape(PATCH, 16, D)

    def keys_of(y, rows):
        keys[:, rows, :] = nn(y[...], wk[...]).astype(BF).reshape(PATCH, 16, D)

    def rows_of(b):
        return pl.ds(pl.multiple_of(16 * b + 16, 16), 16)

    def own(b, out):
        block = raw[b]
        normed(block, rows_of(b), out)
        tokmean[pl.ds(pl.multiple_of(16 * b, 16), 16), :] = nn(avg, block)

    for b in range(8):
        tok_copies[b].wait()
    w_copies[2].wait()
    own(0, y0)

    def norm_pair(i, carry):
        own(2 * i + 1, y1)
        keys_of(y0, rows_of(2 * i))
        own(2 * i + 2, y0)
        keys_of(y1, rows_of(2 * i + 1))
        return carry

    lax.fori_loop(0, 3, norm_pair, 0)
    own(7, y1)
    keys_of(y0, rows_of(6))
    keys_of(y1, rows_of(7))

    scale = math.log2(math.e) / 8.0

    def queries(i, carry):
        x2 = xn[pl.ds(2 * i, 2), 16:16 + COUNT, :].reshape(256, D)
        for c in range(2):
            r = nt(wqvt[512 * c:512 * c + 512], x2) * scale
            for u in range(2):
                for n in range(8):
                    j, h = 2 * c + n // 4, n % 4
                    part = r[64 * n:64 * n + 64, COUNT * u:COUNT * u + COUNT]
                    if h:
                        part = pltpu.roll(part, 32 * h, 1)
                    part = part.astype(BF)
                    for b in range(4):
                        masked = jnp.where(lane_block == (b + h) % 4, part, 0.0)
                        qbd[2 * i + u, j, b, 64 * h:64 * h + 64, :] = masked.astype(BF)
        return carry

    lax.fori_loop(0, 8, queries, 0)

    def values(ga, ra, gb, rb):
        xa = xn[pl.ds(4 * ga, 4), 32 * ra:32 * ra + 32, :].reshape(128, D)
        xb = xn[pl.ds(4 * gb, 4), 32 * rb:32 * rb + 32, :].reshape(128, D)
        x2 = jnp.concatenate([xa, xb], axis=0)
        for c in range(2):
            r = nt(wqvt[D + 512 * c:D + 512 * c + 512], x2).astype(BF)
            vt[ga, 512 * c:512 * c + 512, 128 * ra:128 * ra + 128] = r[:, :128]
            vt[gb, 512 * c:512 * c + 512, 128 * rb:128 * rb + 128] = r[:, 128:]

    def values_inner(g, carry):
        values(g, 1, g, 2)
        return carry

    def values_last(g, carry):
        values(2 * g, 3, 2 * g + 1, 3)
        return carry

    lax.fori_loop(0, 4, values_inner, 0)
    lax.fori_loop(0, 2, values_last, 0)

    halo_copies[0].wait_recv()
    normed(halo[0], pl.ds(0, 16), y0)
    halo_copies[1].wait_recv()
    normed(halo[1], pl.ds(16 + COUNT, 16), y1)
    keys_of(y0, pl.ds(0, 16))
    keys_of(y1, pl.ds(16 + COUNT, 16))

    def values_outer(g, carry):
        values(g, 0, g, 4)
        return carry

    lax.fori_loop(0, 4, values_outer, 0)

    acc[...] = jnp.zeros_like(acc)

    def where_is(u):
        return u // 4, u % 4

    def scores_of(u, out):
        g, j = where_is(u)
        cols = pl.ds(pl.multiple_of(256 * j, 256), 256)
        for q in range(4):
            for b in range(4):
                out[q, b] = nn(keys[4 * g + q, 32 * b:32 * b + 64, cols], qbd[4 * g + q, j, b])

    def softmax_of(src, out):
        for b in range(4):
            mask = bias[b]
            for q in range(4):
                s = src[q, b] + mask
                e = jnp.exp2(s - jnp.max(s, axis=0, keepdims=True))
                e = (e * (1.0 / jnp.sum(e, axis=0, keepdims=True))).astype(BF)
                out[b, 32 * q:32 * q + 32, :] = e[:32]
                out[b, 128 + 32 * q:128 + 32 * q + 32, :] = e[32:]

    def attended_of(u, probs):
        g, j = where_is(u)
        rows = pl.ds(pl.multiple_of(256 * j, 256), 256)
        parts = [nn(vt[g, rows, 128 * b:128 * b + 256], probs[b]) for b in range(4)]
        for h in range(4):
            pick = parts[0][64 * h:64 * h + 64]
            for b in range(1, 4):
                pick = jnp.where(lane_block == (b + h) % 4, parts[b][64 * h:64 * h + 64], pick)
            acc[pl.ds(pl.multiple_of(256 * j + 64 * h, 64), 64), :] += pick

    scores_of(0, st0)
    scores_of(1, st1)
    softmax_of(st0, pr0)

    def attend(i, carry):
        u = 2 * i
        scores_of(u + 2, st0)
        softmax_of(st1, pr1)
        attended_of(u, pr0)
        scores_of(u + 3, st1)
        softmax_of(st0, pr0)
        attended_of(u + 1, pr1)
        return carry

    lax.fori_loop(0, 7, attend, 0)
    softmax_of(st1, pr1)
    attended_of(14, pr0)
    attended_of(15, pr1)

    w_copies[3].wait()
    heads = []
    for h in range(16):
        part = acc[64 * h:64 * h + 64, :]
        heads.append(pltpu.roll(part, 128 - 32 * (h % 4), 1) if h % 4 else part)
    att = jnp.transpose(jnp.concatenate(heads, axis=0) * (1.0 / PATCH)).astype(BF)
    pooled = tokmean[...] + nn(att, wo[...])
    blocks = pooled.reshape(VIDS, PART, D)
    pack[...] = jnp.concatenate([blocks[:, :, :HALF], blocks[:, :, HALF:]], axis=1).astype(BF)

    pooled_copies = [
        pltpu.make_async_remote_copy(
            src_ref=pack.at[peers[k]], dst_ref=got.at[vid],
            send_sem=a_send.at[k], recv_sem=a_recv.at[k],
            device_id={"vid": peers[k]}, device_id_type=MESH,
        )
        for k in range(1, VIDS)
    ]
    near_copies = [
        pltpu.make_async_remote_copy(
            src_ref=pack.at[VIDS - 1], dst_ref=near.at[0],
            send_sem=n_send.at[0], recv_sem=n_recv.at[0],
            device_id={"tm": right}, device_id_type=MESH,
        ),
        pltpu.make_async_remote_copy(
            src_ref=pack.at[0], dst_ref=near.at[1],
            send_sem=n_send.at[1], recv_sem=n_recv.at[1],
            device_id={"tm": left}, device_id_type=MESH,
        ),
    ]
    for copy in pooled_copies + near_copies:
        copy.start()
    got[vid] = pack[vid]

    w_copies[5].wait()
    w_copies[6].wait()
    mine = pooled.astype(BF)
    own_e[:, :D] = nn(mine, wq[...]).astype(BF)
    own_e[:, D:] = nn(mine, wv[...]).astype(BF)
    out_copy = pltpu.make_async_copy(own_e, emb_out, out_sem)
    out_copy.start()

    e = own_e[...]
    near_own = nt(e, e)

    for copy in near_copies + pooled_copies:
        copy.wait_recv()
    seen = jnp.concatenate([got[...], near[...]], axis=0).astype(F32)
    seen = jnp.concatenate([seen[:, :PART], seen[:, PART:]], axis=2)
    seen = seen.reshape((VIDS + 2) * PART, D).astype(BF)
    all_e = jnp.concatenate([nn(seen, wq[...]).astype(BF), nn(seen, wv[...]).astype(BF)], axis=1)
    factor = 8.0 / math.sqrt(E)
    gram = nt(all_e[:COUNT], all_e[:COUNT]) * factor

    frame_here = first + PART * vid + lane % PART
    other = jnp.zeros((COUNT, COUNT), I32)
    for m in range(VIDS):
        other = jnp.where(lane // PART == m, valid[m], other)
    times = count[...]
    neg = jnp.where(frame_here < other, gram, -1e30)
    top = jnp.max(jnp.where(times > 0, neg, -3e38), axis=1, keepdims=True)
    some = jnp.sum(jnp.where(times > 0, times * jnp.exp(jnp.minimum(neg - top, 0.0)), 0.0), axis=1, keepdims=True)
    lse = top + jnp.log(some)
    lse_out[...] = jnp.broadcast_to(lse, (COUNT, 128)).reshape(VIDS, PART, 128)

    back_copies = [
        pltpu.make_async_remote_copy(
            src_ref=lse_out.at[peers[k]], dst_ref=lse_in.at[vid],
            send_sem=b_send.at[k], recv_sem=b_recv.at[k],
            device_id={"vid": peers[k]}, device_id_type=MESH,
        )
        for k in range(1, VIDS)
    ]
    for copy in back_copies:
        copy.start()
    lse_in[vid] = lse_out[vid]

    near_e = nt(all_e[COUNT:], e)
    scores = jnp.concatenate([near_e[:REACH], near_own, near_e[REACH:]], axis=0)
    off = offsets[...]
    here = first + iota((1, COUNT), 1)
    ahead = here + off
    inside = (ahead >= 0) & (ahead < length)
    slot = jnp.where(inside, ahead, here - off) - first + REACH
    pick = iota((COUNT + 2 * REACH, COUNT), 0) == slot
    pos = jnp.sum(jnp.where(pick, scores, 0.0), axis=0, keepdims=True) * factor

    for copy in back_copies:
        copy.wait_recv()
    back = lse_in[...].reshape(COUNT, 128)
    lse_neg = jnp.sum(jnp.where(row == lane, back, 0.0), axis=0, keepdims=True)
    peak = jnp.maximum(pos, lse_neg)
    total = peak + jnp.log(jnp.exp(pos - peak) + jnp.exp(lse_neg - peak))
    loss_out[...] = jnp.where(here < length, total - pos, 0.0)

    for copy in halo_copies + pooled_copies + near_copies + back_copies:
        copy.wait_send()
    out_copy.wait()


def local(tokens, norm_gain, w_qkv, w_out, w_proj, offsets, negatives, valid):
    anywhere = pl.BlockSpec(memory_space=pl.ANY)
    vmem = pl.BlockSpec(memory_space=pltpu.VMEM)
    dma = pltpu.SemaphoreType.DMA
    emb, losses = pl.pallas_call(
        kernel,
        out_shape=(
            jax.ShapeDtypeStruct((COUNT, E), BF),
            jax.ShapeDtypeStruct((1, COUNT), F32),
        ),
        in_specs=[
            pl.BlockSpec(memory_space=pltpu.SMEM), anywhere, vmem, anywhere, anywhere, anywhere, vmem, anywhere,
        ],
        out_specs=(anywhere, vmem),
        scratch_shapes=[
            pltpu.VMEM((8, 256, D), BF),
            pltpu.VMEM((2, 256, D), BF),
            pltpu.VMEM((D, D), BF),
            pltpu.VMEM((D, D), BF),
            pltpu.VMEM((D, D), BF),
            pltpu.VMEM((D, D), BF),
            pltpu.VMEM((VIDS, NEG, COUNT), I32),
            pltpu.VMEM((COUNT, VIDS * NEG), F32),
            pltpu.VMEM((2 * D, D), BF),
            pltpu.VMEM((PATCH, 160, D), BF),
            pltpu.VMEM((PATCH, 160, D), BF),
            pltpu.VMEM((PATCH, 4, 4, 256, 128), BF),
            pltpu.VMEM((4, D, 640), BF),
            pltpu.VMEM((256, D), BF),
            pltpu.VMEM((256, D), BF),
            pltpu.VMEM((4, 64, 128), F32),
            pltpu.VMEM((4, 4, 64, 128), F32),
            pltpu.VMEM((4, 4, 64, 128), F32),
            pltpu.VMEM((4, 256, 128), BF),
            pltpu.VMEM((4, 256, 128), BF),
            pltpu.VMEM((COUNT, D), F32),
            pltpu.VMEM((D, COUNT), F32),
            pltpu.VMEM((VIDS, 16, HALF), BF),
            pltpu.VMEM((VIDS, 16, HALF), BF),
            pltpu.VMEM((2, 16, HALF), BF),
            pltpu.VMEM((COUNT, E), BF),
            pltpu.VMEM((COUNT, COUNT), F32),
            pltpu.VMEM((VIDS, PART, 128), F32),
            pltpu.VMEM((VIDS, PART, 128), F32),
            dma((8,)), dma((7,)), dma, dma((2,)), dma((2,)), dma((VIDS,)), dma((VIDS,)),
            dma((2,)), dma((2,)), dma((VIDS,)), dma((VIDS,)),
        ],
        compiler_params=pltpu.CompilerParams(
            collective_id=0, has_side_effects=True, vmem_limit_bytes=60 * 1024 * 1024
        ),
    )(
        valid,
        tokens.reshape(COUNT * PATCH, D),
        norm_gain.reshape(1, D),
        w_qkv,
        w_out,
        w_proj,
        offsets,
        jnp.swapaxes(negatives, 1, 2),
    )
    return emb.reshape(1, COUNT, E), losses


def solution(mesh):
    placed = (
        P("vid", "tm", None, None),
        P(),
        P(),
        P(),
        P(),
        P("vid", "tm"),
        P(None, "tm", None),
        P(),
    )
    return jax.shard_map(
        local,
        mesh=mesh,
        in_specs=placed,
        out_specs=(P("vid", "tm", None), P("vid", "tm")),
        check_vma=False,
    )
```

```python
import itertools
import math

import jax
import jax.numpy as jnp
from jax import lax
from jax.experimental import pallas as pl
from jax.experimental.pallas import tpu as pltpu
from jax.sharding import PartitionSpec as P

MESH = pl.DeviceIdType.MESH
BF, F32, I32 = jnp.bfloat16, jnp.float32, jnp.int32
D = 1024
E = 2048
PATCH = 16
WINDOW = 16
REACH = 8
COUNT = 128
VIDS = 16
TMS = 8
NEG = 8
PART = COUNT // VIDS
HALF = D // 2


def nn(a, b):
    return lax.dot_general(a, b, (((1,), (0,)), ((), ())), preferred_element_type=F32)


def nt(a, b):
    return lax.dot_general(a, b, (((1,), (1,)), ((), ())), preferred_element_type=F32)


def iota(shape, dim):
    return lax.broadcasted_iota(I32, shape, dim)


def kernel(
    valid, tokens, gain, w_qkv, w_out, w_proj, offsets, negatives,
    emb_out, loss_out,
    raw, halo, wq, wk, wv, wo, negs, negt, wqvt, xn, keys, qt, vt, y0, y1,
    bias, st0, st1, pr0, pr1, tokmean, acc, pack, got, near, own_e, count_out, count, lse_out, lse_in,
    tok_sem, w_sem, out_sem, halo_send, halo_recv, a_send, a_recv, n_send, n_recv, b_send, b_recv, c_send, c_recv,
):
    vid = lax.axis_index("vid")
    tm = lax.axis_index("tm")
    left = lax.rem(tm + TMS - 1, TMS)
    right = lax.rem(tm + 1, TMS)
    across = lax.rem(tm + TMS // 2, TMS)
    peers = [{"vid": lax.rem(vid + k, VIDS), "tm": across} for k in range(VIDS)]
    first = tm * COUNT
    length = valid[vid]

    tok_copies = [
        pltpu.make_async_copy(tokens.at[pl.ds(256 * b, 256)], raw.at[b], tok_sem.at[b])
        for b in range(8)
    ]
    w_copies = [
        pltpu.make_async_copy(src, dst, w_sem.at[i])
        for i, (src, dst) in enumerate(
            [
                (w_qkv.at[:, pl.ds(0, D)], wq),
                (w_qkv.at[:, pl.ds(2 * D, D)], wv),
                (w_qkv.at[:, pl.ds(D, D)], wk),
                (w_out, wo),
                (negatives, negs),
                (w_proj.at[:, pl.ds(0, D)], wq),
                (w_proj.at[:, pl.ds(D, D)], wv),
            ]
        )
    ]
    barrier = pltpu.get_barrier_semaphore()
    for peer in peers:
        pl.semaphore_signal(barrier, inc=1, device_id=peer, device_id_type=MESH)
    for peer in (left, right):
        pl.semaphore_signal(barrier, inc=1, device_id={"tm": peer}, device_id_type=MESH)
    w_copies[0].start()
    tok_copies[0].start()
    w_copies[1].start()
    for copy in tok_copies[1:]:
        copy.start()
    for copy in w_copies[2:5]:
        copy.start()
    r0, r1 = iota((256, 256), 0), iota((256, 256), 1)
    perm = (r1 == (r0 % 16) * 16 + r0 // 16).astype(F32).astype(BF)
    eye = (r0 == r1).astype(F32).astype(BF)
    avg = jnp.where(iota((16, 256), 0) == iota((16, 256), 1) // 16, 1.0 / PATCH, 0.0).astype(BF)

    g0, f0 = iota((64, 128), 0), iota((64, 128), 1) % 32
    for b in range(4):
        frame = g0 + (32 * b - WINDOW)
        query = f0 + 32 * b
        glob = frame + first
        ok = (jnp.abs(frame - query) <= WINDOW) & (glob >= 0) & (glob < TMS * COUNT)
        ok = ok & ((glob < length) | (frame == query))
        bias[b] = jnp.where(ok, 0.0, -1e30)
    lane_block = iota((64, 128), 1) // 32

    w_copies[4].wait()
    lane = iota((COUNT, COUNT), 1)
    row = iota((COUNT, COUNT), 0)
    negt[...] = jnp.transpose(negs[...].reshape(VIDS * NEG, COUNT).astype(F32))
    ids = negt[pl.ds(pl.multiple_of(PART * vid, PART), PART), :]
    ids = jnp.concatenate([ids] * VIDS, axis=0)
    times = jnp.zeros((COUNT, COUNT), F32)
    for k in range(NEG):
        one = jnp.sum(jnp.where(lane == row // PART * NEG + k, ids, 0.0), axis=1, keepdims=True)
        times += (one * PART + (row % PART).astype(F32) == lane.astype(F32)).astype(F32)
    count_out[...] = times

    w_copies[0].wait()

    def flip(src, base):
        def body(i, carry):
            a = pl.multiple_of(i * 256, 256)
            for c in range(4):
                block = nt(eye, src[256 * c:256 * c + 256, pl.ds(a, 256)])
                wqvt[pl.ds(base + a, 256), 256 * c:256 * c + 256] = block.astype(BF)
            return carry
        lax.fori_loop(0, 4, body, 0)

    flip(wq, 0)
    w_copies[1].wait()
    flip(wv, D)
    w_copies[5].start()
    w_copies[6].start()

    pl.semaphore_wait(barrier, VIDS + 2)

    halo_copies = [
        pltpu.make_async_remote_copy(
            src_ref=tokens.at[pl.ds(256 * 7, 256)], dst_ref=halo.at[0],
            send_sem=halo_send.at[0], recv_sem=halo_recv.at[0],
            device_id={"tm": right}, device_id_type=MESH,
        ),
        pltpu.make_async_remote_copy(
            src_ref=tokens.at[pl.ds(0, 256)], dst_ref=halo.at[1],
            send_sem=halo_send.at[1], recv_sem=halo_recv.at[1],
            device_id={"tm": left}, device_id_type=MESH,
        ),
    ]
    for copy in halo_copies:
        copy.start()

    count_copy = pltpu.make_async_remote_copy(
        src_ref=count_out, dst_ref=count, send_sem=c_send, recv_sem=c_recv, device_id=peers[0], device_id_type=MESH,
    )
    count_copy.start()

    def normed(block, out, rows=(0, 1, 2, 3)):
        for c in rows:
            for n in range(4):
                at = 64 * c + 16 * n
                x = block[at:at + 16, :].astype(F32)
                mean = jnp.sum(x * x, axis=1, keepdims=True) * (1.0 / D)
                out[at:at + 16, :] = (x * lax.rsqrt(mean + 1e-5) * gain[...]).astype(BF)
            yield

    def permuted(y, rows):
        for c in range(4):
            part = nn(perm, y[:, 256 * c:256 * c + 256]).astype(BF)
            xn[:, rows, 256 * c:256 * c + 256] = part.reshape(PATCH, 16, 256)
            yield

    def averaged(b):
        tokmean[pl.ds(pl.multiple_of(16 * b, 16), 16), :] = nn(avg, raw[b])
        yield

    def rows_of(b):
        return pl.ds(pl.multiple_of(16 * b + 16, 16), 16)

    def weave(*jobs):
        for _ in itertools.zip_longest(*jobs):
            pass

    for b in range(8):
        tok_copies[b].wait()
    weave(normed(raw.at[0], y0))

    def norm_pair(i, carry):
        b = 2 * i
        weave(permuted(y0, rows_of(b)), normed(raw.at[b + 1], y1), averaged(b))
        weave(permuted(y1, rows_of(b + 1)), normed(raw.at[b + 2], y0), averaged(b + 1))
        return carry

    lax.fori_loop(0, 3, norm_pair, 0)
    weave(permuted(y0, rows_of(6)), normed(raw.at[7], y1), averaged(6))
    weave(permuted(y1, rows_of(7)), averaged(7))

    scale = math.log2(math.e) / 8.0

    def queries(i, carry):
        x2 = xn[pl.ds(2 * i, 2), 16:16 + COUNT, :].reshape(256, D)
        for c in range(2):
            r = nt(wqvt[512 * c:512 * c + 512], x2) * scale
            for u in range(2):
                for n in range(8):
                    part = r[64 * n:64 * n + 64, COUNT * u:COUNT * u + COUNT]
                    if n % 4:
                        part = pltpu.roll(part, 32 * (n % 4), 1)
                    qt[2 * i + u, 512 * c + 64 * n:512 * c + 64 * n + 64, :] = part.astype(BF)
        return carry

    lax.fori_loop(0, 8, queries, 0)

    def values(ga, ra, gb, rb):
        xa = xn[pl.ds(4 * ga, 4), 32 * ra:32 * ra + 32, :].reshape(128, D)
        xb = xn[pl.ds(4 * gb, 4), 32 * rb:32 * rb + 32, :].reshape(128, D)
        x2 = jnp.concatenate([xa, xb], axis=0)
        for c in range(2):
            r = nt(wqvt[D + 512 * c:D + 512 * c + 512], x2).astype(BF)
            vt[ga, 512 * c:512 * c + 512, 128 * ra:128 * ra + 128] = r[:, :128]
            vt[gb, 512 * c:512 * c + 512, 128 * rb:128 * rb + 128] = r[:, 128:]

    def values_inner(g, carry):
        values(g, 1, g, 2)
        return carry

    def values_last(g, carry):
        values(2 * g, 3, 2 * g + 1, 3)
        return carry

    lax.fori_loop(0, 4, values_inner, 0)
    lax.fori_loop(0, 2, values_last, 0)

    halo_copies[0].wait_recv()
    halo_copies[1].wait_recv()
    weave(normed(halo.at[0], y0))
    weave(permuted(y0, pl.ds(0, 16)), normed(halo.at[1], y1))
    weave(permuted(y1, pl.ds(16 + COUNT, 16)))

    w_copies[2].wait()

    def project_keys(i, carry):
        rows = pl.ds(pl.multiple_of(512 * i, 512), 512)
        for c in range(2):
            keys[rows, 512 * c:512 * c + 512] = nn(xn.reshape(PATCH * 160, D)[rows, :], wk[:, 512 * c:512 * c + 512]).astype(BF)
        return carry

    lax.fori_loop(0, 5, project_keys, 0)

    def values_outer(g, carry):
        values(g, 0, g, 4)
        return carry

    lax.fori_loop(0, 4, values_outer, 0)

    acc[...] = jnp.zeros_like(acc)

    def where_is(u):
        return u // 2, pl.ds(pl.multiple_of(512 * (u % 2), 512), 512)

    diagonal = [jnp.concatenate([lane_block == (b + h) % 4 for h in range(4)] * 2, axis=0) for b in range(4)]

    def scores_of(u, out):
        g, cols = where_is(u)
        for q in range(4):
            p = 4 * g + q
            for b in range(4):
                q8 = qt[p, cols, :]
                q8 = jnp.where(diagonal[b], q8, jnp.zeros_like(q8))
                k8 = keys[pl.ds(pl.multiple_of(160 * p + 32 * b, 32), 64), cols]
                r = nn(
                    jnp.concatenate([k8[:, :256], k8[:, 256:]], axis=0),
                    jnp.concatenate([q8[:256], q8[256:]], axis=1),
                )
                out[q, b, :, :128] = r[:64, :128]
                out[q, b, :, 128:] = r[64:, 128:]
                yield

    def softmax_of(src, out):
        for q in range(4):
            for b in range(4):
                for j in range(2):
                    s = src[q, b, :, 128 * j:128 * j + 128] + bias[b]
                    e = jnp.exp2(s - jnp.max(s, axis=0, keepdims=True))
                    e = (e * (1.0 / jnp.sum(e, axis=0, keepdims=True))).astype(BF)
                    out[b, 32 * q:32 * q + 32, 128 * j:128 * j + 128] = e[:32]
                    out[b, 128 + 32 * q:128 + 32 * q + 32, 128 * j:128 * j + 128] = e[32:]
                yield

    def attended_of(u, probs):
        g, rows = where_is(u)
        for b in range(4):
            r = nn(vt[g, rows, 128 * b:128 * b + 256], probs[b])
            for j in range(2):
                for h in range(4):
                    at = 256 * j + 64 * h
                    part = r[at:at + 64, 128 * j:128 * j + 128]
                    where = pl.ds(pl.multiple_of(512 * (u % 2) + at, 64), 64)
                    acc[where, :] += jnp.where(lane_block == (b + h) % 4, part, 0.0)
            for _ in range(4):
                yield

    weave(scores_of(0, st0))
    weave(scores_of(1, st1), softmax_of(st0, pr0))

    def attend(i, carry):
        u = 2 * i
        weave(scores_of(u + 2, st0), softmax_of(st1, pr1), attended_of(u, pr0))
        weave(scores_of(u + 3, st1), softmax_of(st0, pr0), attended_of(u + 1, pr1))
        return carry

    lax.fori_loop(0, 3, attend, 0)
    weave(softmax_of(st1, pr1), attended_of(6, pr0))
    weave(attended_of(7, pr1))

    w_copies[3].wait()
    heads = []
    for h in range(16):
        part = acc[64 * h:64 * h + 64, :]
        heads.append(pltpu.roll(part, 128 - 32 * (h % 4), 1) if h % 4 else part)
    att = jnp.transpose(jnp.concatenate(heads, axis=0) * (1.0 / PATCH)).astype(BF)
    pooled = tokmean[...] + nn(att, wo[...])
    blocks = pooled.reshape(VIDS, PART, D)
    pack[...] = jnp.concatenate([blocks[:, :, :HALF], blocks[:, :, HALF:]], axis=1).astype(BF)

    pooled_copies = [
        pltpu.make_async_remote_copy(
            src_ref=pack.at[peers[k]["vid"]], dst_ref=got.at[vid],
            send_sem=a_send, recv_sem=a_recv,
            device_id=peers[k], device_id_type=MESH,
        )
        for k in range(VIDS)
    ]
    near_copies = [
        pltpu.make_async_remote_copy(
            src_ref=pack.at[VIDS - 1], dst_ref=near.at[0],
            send_sem=n_send.at[0], recv_sem=n_recv.at[0],
            device_id={"tm": right}, device_id_type=MESH,
        ),
        pltpu.make_async_remote_copy(
            src_ref=pack.at[0], dst_ref=near.at[1],
            send_sem=n_send.at[1], recv_sem=n_recv.at[1],
            device_id={"tm": left}, device_id_type=MESH,
        ),
    ]
    for copy in pooled_copies + near_copies:
        copy.start()

    w_copies[5].wait()
    w_copies[6].wait()
    mine = pooled.astype(BF)
    own_e[:, :D] = nn(mine, wq[...]).astype(BF)
    own_e[:, D:] = nn(mine, wv[...]).astype(BF)
    out_copy = pltpu.make_async_copy(own_e, emb_out, out_sem)
    out_copy.start()

    e = own_e[...]
    near_own = nt(e, e)

    for copy in near_copies:
        copy.wait_recv()
    pltpu.make_async_copy(got, got, a_recv).wait()
    seen = jnp.concatenate([got[...], near[...]], axis=0).astype(F32)
    seen = jnp.concatenate([seen[:, :PART], seen[:, PART:]], axis=2)
    seen = seen.reshape((VIDS + 2) * PART, D).astype(BF)
    all_e = jnp.concatenate([nn(seen, wq[...]).astype(BF), nn(seen, wv[...]).astype(BF)], axis=1)
    factor = 8.0 / math.sqrt(E)
    gram = nt(all_e[:COUNT], all_e[:COUNT]) * factor

    frame_here = across * COUNT + PART * vid + lane % PART
    other = jnp.zeros((COUNT, COUNT), I32)
    for m in range(VIDS):
        other = jnp.where(lane // PART == m, valid[m], other)
    count_copy.wait_recv()
    times = count[...]
    neg = jnp.where(frame_here < other, gram, -1e30)
    top = jnp.max(jnp.where(times > 0, neg, -3e38), axis=1, keepdims=True)
    some = jnp.sum(jnp.where(times > 0, times * jnp.exp(jnp.minimum(neg - top, 0.0)), 0.0), axis=1, keepdims=True)
    lse = top + jnp.log(some)
    lse_out[...] = jnp.broadcast_to(lse, (COUNT, 128)).reshape(VIDS, PART, 128)

    back_copies = [
        pltpu.make_async_remote_copy(
            src_ref=lse_out.at[peers[k]["vid"]], dst_ref=lse_in.at[vid],
            send_sem=b_send, recv_sem=b_recv,
            device_id=peers[k], device_id_type=MESH,
        )
        for k in range(VIDS)
    ]
    for copy in back_copies:
        copy.start()

    near_e = nt(all_e[COUNT:], e)
    scores = jnp.concatenate([near_e[:REACH], near_own, near_e[REACH:]], axis=0)
    off = offsets[...]
    here = first + iota((1, COUNT), 1)
    ahead = here + off
    inside = (ahead >= 0) & (ahead < length)
    slot = jnp.where(inside, ahead, here - off) - first + REACH
    pick = iota((COUNT + 2 * REACH, COUNT), 0) == slot
    pos = jnp.sum(jnp.where(pick, scores, 0.0), axis=0, keepdims=True) * factor

    pltpu.make_async_copy(lse_in, lse_in, b_recv).wait()
    back = lse_in[...].reshape(COUNT, 128)
    lse_neg = jnp.sum(jnp.where(row == lane, back, 0.0), axis=0, keepdims=True)
    peak = jnp.maximum(pos, lse_neg)
    total = peak + jnp.log(jnp.exp(pos - peak) + jnp.exp(lse_neg - peak))
    loss_out[...] = jnp.where(here < length, total - pos, 0.0)

    for copy in halo_copies + near_copies + [count_copy]:
        copy.wait_send()
    pltpu.make_async_copy(pack, pack, a_send).wait()
    pltpu.make_async_copy(lse_out, lse_out, b_send).wait()
    out_copy.wait()


def hand_over(emb, losses, emb_out, loss_out):
    emb_out[...] = emb[...]
    loss_out[...] = losses[...]


def local(tokens, norm_gain, w_qkv, w_out, w_proj, offsets, negatives, valid):
    anywhere = pl.BlockSpec(memory_space=pl.ANY)
    vmem = pl.BlockSpec(memory_space=pltpu.VMEM)
    dma = pltpu.SemaphoreType.DMA
    emb, losses = pl.pallas_call(
        kernel,
        out_shape=(
            jax.ShapeDtypeStruct((COUNT, E), BF),
            jax.ShapeDtypeStruct((1, COUNT), F32),
        ),
        in_specs=[
            pl.BlockSpec(memory_space=pltpu.SMEM), anywhere, vmem, anywhere, anywhere, anywhere, vmem, anywhere,
        ],
        out_specs=(anywhere, vmem),
        scratch_shapes=[
            pltpu.VMEM((8, 256, D), BF),
            pltpu.VMEM((2, 256, D), BF),
            pltpu.VMEM((D, D), BF),
            pltpu.VMEM((D, D), BF),
            pltpu.VMEM((D, D), BF),
            pltpu.VMEM((D, D), BF),
            pltpu.VMEM((VIDS, NEG, COUNT), I32),
            pltpu.VMEM((COUNT, VIDS * NEG), F32),
            pltpu.VMEM((2 * D, D), BF),
            pltpu.VMEM((PATCH, 160, D), BF),
            pltpu.VMEM((PATCH * 160, D), BF),
            pltpu.VMEM((PATCH, D, COUNT), BF),
            pltpu.VMEM((4, D, 640), BF),
            pltpu.VMEM((256, D), BF),
            pltpu.VMEM((256, D), BF),
            pltpu.VMEM((4, 64, 128), F32),
            pltpu.VMEM((4, 4, 64, 256), F32),
            pltpu.VMEM((4, 4, 64, 256), F32),
            pltpu.VMEM((4, 256, 256), BF),
            pltpu.VMEM((4, 256, 256), BF),
            pltpu.VMEM((COUNT, D), F32),
            pltpu.VMEM((D, COUNT), F32),
            pltpu.VMEM((VIDS, 16, HALF), BF),
            pltpu.VMEM((VIDS, 16, HALF), BF),
            pltpu.VMEM((2, 16, HALF), BF),
            pltpu.VMEM((COUNT, E), BF),
            pltpu.VMEM((COUNT, COUNT), F32),
            pltpu.VMEM((COUNT, COUNT), F32),
            pltpu.VMEM((VIDS, PART, 128), F32),
            pltpu.VMEM((VIDS, PART, 128), F32),
            dma((8,)), dma((7,)), dma, dma((2,)), dma((2,)), dma, dma, dma((2,)), dma((2,)), dma, dma, dma, dma,
        ],
        compiler_params=pltpu.CompilerParams(
            collective_id=0, has_side_effects=True, vmem_limit_bytes=60 * 1024 * 1024
        ),
    )(
        valid,
        tokens.reshape(COUNT * PATCH, D),
        norm_gain.reshape(1, D),
        w_qkv,
        w_out,
        w_proj,
        offsets,
        jnp.swapaxes(negatives, 1, 2),
    )
    emb, losses = pl.pallas_call(
        hand_over,
        out_shape=(
            jax.ShapeDtypeStruct((COUNT, E), BF),
            jax.ShapeDtypeStruct((1, COUNT), F32),
        ),
        in_specs=[vmem, vmem],
        out_specs=(vmem, vmem),
    )(emb, losses)
    return emb.reshape(1, COUNT, E), losses


def solution(mesh):
    placed = (
        P("vid", "tm", None, None),
        P(),
        P(),
        P(),
        P(),
        P("vid", "tm"),
        P(None, "tm", None),
        P(),
    )
    return jax.shard_map(
        local,
        mesh=mesh,
        in_specs=placed,
        out_specs=(P("vid", "tm", None), P("vid", "tm")),
        check_vma=False,
    )
```

```python
import itertools
import math

import jax
import jax.numpy as jnp
from jax import lax
from jax.experimental import pallas as pl
from jax.experimental.pallas import tpu as pltpu
from jax.sharding import PartitionSpec as P

MESH = pl.DeviceIdType.MESH
BF, F32, I32 = jnp.bfloat16, jnp.float32, jnp.int32
D = 1024
E = 2048
PATCH = 16
WINDOW = 16
REACH = 8
COUNT = 128
VIDS = 16
TMS = 8
NEG = 8
PART = COUNT // VIDS
HALF = D // 2


def nn(a, b):
    return lax.dot_general(a, b, (((1,), (0,)), ((), ())), preferred_element_type=F32)


def nt(a, b):
    return lax.dot_general(a, b, (((1,), (1,)), ((), ())), preferred_element_type=F32)


def iota(shape, dim):
    return lax.broadcasted_iota(I32, shape, dim)


def kernel(
    valid, tokens, gain, w_qkv, w_out, w_proj, offsets, negatives,
    emb_out, loss_out,
    perm, eye, avg, raw, halo, wq, wk, wv, wo, wp, negs, negt, wvt, xn, keys, queries, vt, y0, y1,
    bias, st0, st1, pr0, pr1, tokmean, acc, pack, got, near, own_e, count_out, count, lse_out, lse_in,
    tok_sem, w_sem, out_sem, halo_send, halo_recv, a_send, a_recv, n_send, n_recv, b_send, b_recv, c_send, c_recv,
):
    vid = lax.axis_index("vid")
    tm = lax.axis_index("tm")
    left = lax.rem(tm + TMS - 1, TMS)
    right = lax.rem(tm + 1, TMS)
    across = lax.rem(tm + TMS // 2, TMS)
    y_hi, z, core = vid // 8, vid // 2 % 4, vid % 2
    peers = [
        {"vid": (y_hi + dy) % 2 * 8 + (z + dz) % 4 * 2 + (core + dc) % 2, "tm": across}
        for dz in (2, 1, 3, 0) for dy in (1, 0) for dc in (1, 0)
    ]
    first = tm * COUNT
    length = valid[vid]

    tok_copies = [
        pltpu.make_async_copy(tokens.at[pl.ds(256 * b, 256)], raw.at[b], tok_sem.at[b])
        for b in range(8)
    ]
    w_copies = [
        pltpu.make_async_copy(src, dst, w_sem.at[i])
        for i, (src, dst) in enumerate(
            [
                (w_qkv.at[:, pl.ds(2 * D, D)], wv),
                (negatives, negs),
                (w_qkv.at[:, pl.ds(0, D)], wq),
                (w_qkv.at[:, pl.ds(D, D)], wk),
                (w_proj, wp),
            ]
        )
    ]
    out_copies = [
        pltpu.make_async_copy(
            w_out.at[pl.ds(256 * (2 * jp + j2) + 64 * h, 64)],
            wo.at[pl.ds(512 * jp + 128 * h + 64 * j2, 64)],
            w_sem.at[5],
        )
        for jp in range(2) for h in range(4) for j2 in range(2)
    ]
    barrier = pltpu.get_barrier_semaphore()
    for peer in peers:
        pl.semaphore_signal(barrier, inc=1, device_id=peer, device_id_type=MESH)
    for peer in (left, right):
        pl.semaphore_signal(barrier, inc=1, device_id={"tm": peer}, device_id_type=MESH)
    w_copies[1].start()
    tok_copies[0].start()
    w_copies[0].start()
    for copy in tok_copies[1:] + w_copies[2:] + out_copies:
        copy.start()

    r0, r1 = iota((256, 256), 0), iota((256, 256), 1)
    perm[...] = (r1 == (r0 % 16) * 16 + r0 // 16).astype(F32).astype(BF)
    eye[...] = (r0 == r1).astype(F32).astype(BF)
    avg[...] = jnp.where(iota((16, 256), 0) == iota((16, 256), 1) // 16, 1.0 / PATCH, 0.0).astype(BF)

    g0, f0 = iota((64, 128), 0), iota((64, 128), 1) % 32
    for b in range(4):
        frame = g0 + (32 * b - WINDOW)
        query = f0 + 32 * b
        glob = frame + first
        ok = (jnp.abs(frame - query) <= WINDOW) & (glob >= 0) & (glob < TMS * COUNT)
        ok = ok & ((glob < length) | (frame == query))
        bias[b] = jnp.where(ok, 0.0, -1e30)
    lane_block = iota((64, 128), 1) // 32

    w_copies[1].wait()
    lane = iota((COUNT, COUNT), 1)
    row = iota((COUNT, COUNT), 0)
    negt[...] = jnp.transpose(negs[...].reshape(VIDS * NEG, COUNT).astype(F32))
    ids = negt[pl.ds(pl.multiple_of(PART * vid, PART), PART), :]
    ids = jnp.concatenate([ids] * VIDS, axis=0)
    times = jnp.zeros((COUNT, COUNT), F32)
    for k in range(NEG):
        one = jnp.sum(jnp.where(lane == row // PART * NEG + k, ids, 0.0), axis=1, keepdims=True)
        times += (one * PART + (row % PART).astype(F32) == lane.astype(F32)).astype(F32)
    count_out[...] = times

    pl.semaphore_wait(barrier, VIDS + 2)

    halo_copies = [
        pltpu.make_async_remote_copy(
            src_ref=tokens.at[pl.ds(256 * 7, 256)], dst_ref=halo.at[0],
            send_sem=halo_send.at[0], recv_sem=halo_recv.at[0],
            device_id={"tm": right}, device_id_type=MESH,
        ),
        pltpu.make_async_remote_copy(
            src_ref=tokens.at[pl.ds(0, 256)], dst_ref=halo.at[1],
            send_sem=halo_send.at[1], recv_sem=halo_recv.at[1],
            device_id={"tm": left}, device_id_type=MESH,
        ),
    ]
    for copy in halo_copies:
        copy.start()

    count_copy = pltpu.make_async_remote_copy(
        src_ref=count_out, dst_ref=count, send_sem=c_send, recv_sem=c_recv, device_id=peers[-1], device_id_type=MESH,
    )
    count_copy.start()

    def normed(block, out, rows=(0, 1, 2, 3)):
        for c in rows:
            for n in range(4):
                at = 64 * c + 16 * n
                x = block[at:at + 16, :].astype(F32)
                mean = jnp.sum(x * x, axis=1, keepdims=True) * (1.0 / D)
                out[at:at + 16, :] = (x * lax.rsqrt(mean + 1e-5) * gain[...]).astype(BF)
            yield

    def permuted(y, rows):
        for c in range(4):
            part = nn(perm[...], y[:, 256 * c:256 * c + 256]).astype(BF)
            xn[:, rows, 256 * c:256 * c + 256] = part.reshape(PATCH, 16, 256)
            yield

    def averaged(b):
        tokmean[pl.ds(pl.multiple_of(16 * b, 16), 16), :] = nn(avg[...], raw[b])
        yield

    def rows_of(b):
        return pl.ds(pl.multiple_of(16 * b + 16, 16), 16)

    def flip(a):
        for c in range(4):
            block = nt(eye[...], wv[256 * c:256 * c + 256, pl.ds(a, 256)])
            wvt[pl.ds(a, 256), 256 * c:256 * c + 256] = block.astype(BF)
            yield

    def weave(*jobs):
        for _ in itertools.zip_longest(*jobs):
            pass

    def arrived(b):
        pltpu.make_async_copy(tokens.at[pl.ds(0, 256)], raw.at[b], tok_sem.at[b]).wait()

    arrived(0)
    weave(normed(raw.at[0], y0))
    w_copies[0].wait()

    def norm_pair(i, carry):
        b = 2 * i
        arrived(b + 1)
        arrived(b + 2)
        weave(permuted(y0, rows_of(b)), normed(raw.at[b + 1], y1), averaged(b), flip(pl.multiple_of(256 * i, 256)))
        weave(permuted(y1, rows_of(b + 1)), normed(raw.at[b + 2], y0), averaged(b + 1))
        return carry

    lax.fori_loop(0, 3, norm_pair, 0)
    arrived(7)
    weave(permuted(y0, rows_of(6)), normed(raw.at[7], y1), averaged(6), flip(768))
    weave(permuted(y1, rows_of(7)), averaged(7))

    w_copies[2].wait()
    scale = math.log2(math.e) / 8.0

    def project_queries(i, carry):
        rows = pl.ds(pl.multiple_of(512 * i, 512), 512)
        x = xn[pl.ds(4 * i, 4), 16:16 + COUNT, :].reshape(512, D)
        for c in range(2):
            queries[rows, 512 * c:512 * c + 512] = (nn(x, wq[:, 512 * c:512 * c + 512]) * scale).astype(BF)
        return carry

    lax.fori_loop(0, 4, project_queries, 0)

    def values(ga, ra, gb, rb):
        xa = xn[pl.ds(4 * ga, 4), 32 * ra:32 * ra + 32, :].reshape(128, D)
        xb = xn[pl.ds(4 * gb, 4), 32 * rb:32 * rb + 32, :].reshape(128, D)
        x2 = jnp.concatenate([xa, xb], axis=0)
        for c in range(2):
            r = nt(wvt[512 * c:512 * c + 512], x2).astype(BF)
            vt[ga, 512 * c:512 * c + 512, 128 * ra:128 * ra + 128] = r[:, :128]
            vt[gb, 512 * c:512 * c + 512, 128 * rb:128 * rb + 128] = r[:, 128:]
            yield

    def values_inner(i, carry):
        weave(values(2 * i, 1, 2 * i, 2))
        weave(values(2 * i + 1, 1, 2 * i + 1, 2))
        return carry

    lax.fori_loop(0, 2, values_inner, 0)

    halo_copies[0].wait_recv()
    halo_copies[1].wait_recv()
    weave(values(0, 3, 1, 3), normed(halo.at[0], y0))
    weave(values(2, 3, 3, 3), normed(halo.at[1], y1))
    weave(permuted(y0, pl.ds(0, 16)), permuted(y1, pl.ds(16 + COUNT, 16)))

    w_copies[3].wait()

    def project_keys(i, carry):
        rows = pl.ds(pl.multiple_of(512 * i, 512), 512)
        for c in range(2):
            keys[rows, 512 * c:512 * c + 512] = nn(xn.reshape(PATCH * 160, D)[rows, :], wk[:, 512 * c:512 * c + 512]).astype(BF)
        return carry

    lax.fori_loop(0, 5, project_keys, 0)

    def values_outer(i, carry):
        weave(values(2 * i, 0, 2 * i, 4))
        weave(values(2 * i + 1, 0, 2 * i + 1, 4))
        return carry

    lax.fori_loop(0, 2, values_outer, 0)

    acc[...] = jnp.zeros_like(acc)

    def where_is(u):
        return u // 2, pl.ds(pl.multiple_of(512 * (u % 2), 512), 512)

    head_lanes = [iota((32, 256), 1) // 64 == h for h in range(4)]

    def diagonal(x):
        return [jnp.where(head_lanes[h], x, jnp.zeros_like(x)) for h in range(4)]

    def scores_of(u, out):
        g, cols = where_is(u)
        for q in range(4):
            p = 4 * g + q
            for b in range(4):
                q8 = queries[pl.ds(pl.multiple_of(COUNT * p + 32 * b, 32), 32), cols]
                k8 = keys[pl.ds(pl.multiple_of(160 * p + 32 * b, 32), 64), cols]
                r = nt(
                    jnp.concatenate([k8[:, :256], k8[:, 256:]], axis=0),
                    jnp.concatenate(diagonal(q8[:, :256]) + diagonal(q8[:, 256:]), axis=0),
                )
                out[q, b, :, :128] = r[:64, :128]
                out[q, b, :, 128:] = r[64:, 128:]
                yield

    def softmax_of(src, out):
        for q in range(4):
            for b in range(4):
                for j in range(2):
                    s = src[q, b, :, 128 * j:128 * j + 128] + bias[b]
                    e = jnp.exp2(s - jnp.max(s, axis=0, keepdims=True))
                    e = (e * (1.0 / jnp.sum(e, axis=0, keepdims=True))).astype(BF)
                    out[b, 32 * q:32 * q + 32, 128 * j:128 * j + 128] = e[:32]
                    out[b, 128 + 32 * q:128 + 32 * q + 32, 128 * j:128 * j + 128] = e[32:]
                yield

    def attended_of(u, probs):
        g, rows = where_is(u)
        for b in range(4):
            for j in range(2):
                r = nn(vt[g, pl.ds(pl.multiple_of(512 * (u % 2) + 256 * j, 256), 256), 128 * b:128 * b + 256], probs[b, :, 128 * j:128 * j + 128])
                part = r[:64]
                for h in range(1, 4):
                    part = jnp.where(lane_block == h, r[64 * h:64 * h + 64], part)
                acc[u % 2, b, 64 * j:64 * j + 64, :] += part
                yield
                yield

    weave(scores_of(0, st0))
    weave(scores_of(1, st1), softmax_of(st0, pr0))

    def attend(i, carry):
        u = 2 * i
        weave(scores_of(u + 2, st0), softmax_of(st1, pr1), attended_of(u, pr0))
        weave(scores_of(u + 3, st1), softmax_of(st0, pr0), attended_of(u + 1, pr1))
        return carry

    lax.fori_loop(0, 3, attend, 0)
    weave(softmax_of(st1, pr1), attended_of(6, pr0))
    weave(attended_of(7, pr1))

    pltpu.make_async_copy(w_out, wo, w_sem.at[5]).wait()
    att = []
    for b in range(4):
        turned = [jnp.transpose(acc[jp, b] * (1.0 / PATCH)).astype(BF) for jp in range(2)]
        att.append(jnp.concatenate([t[32 * h:32 * h + 32] for t in turned for h in range(4)], axis=1))
    pooled = tokmean[...] + nn(jnp.concatenate(att, axis=0), wo[...])
    blocks = pooled.reshape(VIDS, PART, D)
    pack[...] = jnp.concatenate([blocks[:, :, :HALF], blocks[:, :, HALF:]], axis=1).astype(BF)

    pooled_copies = [
        pltpu.make_async_remote_copy(
            src_ref=pack.at[peers[k]["vid"]], dst_ref=got.at[vid],
            send_sem=a_send, recv_sem=a_recv,
            device_id=peers[k], device_id_type=MESH,
        )
        for k in range(VIDS)
    ]
    near_copies = [
        pltpu.make_async_remote_copy(
            src_ref=pack.at[VIDS - 1], dst_ref=near.at[0],
            send_sem=n_send.at[0], recv_sem=n_recv.at[0],
            device_id={"tm": right}, device_id_type=MESH,
        ),
        pltpu.make_async_remote_copy(
            src_ref=pack.at[0], dst_ref=near.at[1],
            send_sem=n_send.at[1], recv_sem=n_recv.at[1],
            device_id={"tm": left}, device_id_type=MESH,
        ),
    ]
    for copy in pooled_copies + near_copies:
        copy.start()

    w_copies[4].wait()
    own_e[...] = nn(pooled.astype(BF), wp[...]).astype(BF)
    out_copy = pltpu.make_async_copy(own_e, emb_out, out_sem)
    out_copy.start()

    e = own_e[...]
    near_own = nt(e, e)

    for copy in near_copies:
        copy.wait_recv()
    pltpu.make_async_copy(got, got, a_recv).wait()
    seen = jnp.concatenate([got[...], near[...]], axis=0).astype(F32)
    seen = jnp.concatenate([seen[:, :PART], seen[:, PART:]], axis=2)
    seen = seen.reshape((VIDS + 2) * PART, D).astype(BF)
    all_e = nn(seen, wp[...]).astype(BF)
    factor = 8.0 / math.sqrt(E)
    gram = nt(all_e[:COUNT], all_e[:COUNT]) * factor

    frame_here = across * COUNT + PART * vid + lane % PART
    other = jnp.zeros((COUNT, COUNT), I32)
    for m in range(VIDS):
        other = jnp.where(lane // PART == m, valid[m], other)
    count_copy.wait_recv()
    times = count[...]
    neg = jnp.where(frame_here < other, gram, -1e30)
    top = jnp.max(jnp.where(times > 0, neg, -3e38), axis=1, keepdims=True)
    some = jnp.sum(jnp.where(times > 0, times * jnp.exp(jnp.minimum(neg - top, 0.0)), 0.0), axis=1, keepdims=True)
    lse = top + jnp.log(some)
    lse_out[...] = jnp.broadcast_to(lse, (COUNT, 128)).reshape(VIDS, PART, 128)

    back_copies = [
        pltpu.make_async_remote_copy(
            src_ref=lse_out.at[peers[k]["vid"]], dst_ref=lse_in.at[vid],
            send_sem=b_send, recv_sem=b_recv,
            device_id=peers[k], device_id_type=MESH,
        )
        for k in range(VIDS)
    ]
    for copy in back_copies:
        copy.start()

    near_e = nt(all_e[COUNT:], e)
    scores = jnp.concatenate([near_e[:REACH], near_own, near_e[REACH:]], axis=0)
    off = offsets[...]
    here = first + iota((1, COUNT), 1)
    ahead = here + off
    inside = (ahead >= 0) & (ahead < length)
    slot = jnp.where(inside, ahead, here - off) - first + REACH
    pick = iota((COUNT + 2 * REACH, COUNT), 0) == slot
    pos = jnp.sum(jnp.where(pick, scores, 0.0), axis=0, keepdims=True) * factor

    pltpu.make_async_copy(lse_in, lse_in, b_recv).wait()
    back = lse_in[...].reshape(COUNT, 128)
    lse_neg = jnp.sum(jnp.where(row == lane, back, 0.0), axis=0, keepdims=True)
    peak = jnp.maximum(pos, lse_neg)
    total = peak + jnp.log(jnp.exp(pos - peak) + jnp.exp(lse_neg - peak))
    loss_out[...] = jnp.where(here < length, total - pos, 0.0)

    for copy in halo_copies + near_copies + [count_copy]:
        copy.wait_send()
    pltpu.make_async_copy(pack, pack, a_send).wait()
    pltpu.make_async_copy(lse_out, lse_out, b_send).wait()
    out_copy.wait()


def hand_over(emb, losses, emb_out, loss_out):
    emb_out[...] = emb[...]
    loss_out[...] = losses[...]


def local(tokens, norm_gain, w_qkv, w_out, w_proj, offsets, negatives, valid):
    anywhere = pl.BlockSpec(memory_space=pl.ANY)
    vmem = pl.BlockSpec(memory_space=pltpu.VMEM)
    dma = pltpu.SemaphoreType.DMA
    emb, losses = pl.pallas_call(
        kernel,
        out_shape=(
            jax.ShapeDtypeStruct((COUNT, E), BF),
            jax.ShapeDtypeStruct((1, COUNT), F32),
        ),
        in_specs=[
            pl.BlockSpec(memory_space=pltpu.SMEM), anywhere, vmem, anywhere, anywhere, anywhere, vmem, anywhere,
        ],
        out_specs=(anywhere, vmem),
        scratch_shapes=[
            pltpu.VMEM((256, 256), BF),
            pltpu.VMEM((256, 256), BF),
            pltpu.VMEM((16, 256), BF),
            pltpu.VMEM((8, 256, D), BF),
            pltpu.VMEM((2, 256, D), BF),
            pltpu.VMEM((D, D), BF),
            pltpu.VMEM((D, D), BF),
            pltpu.VMEM((D, D), BF),
            pltpu.VMEM((D, D), BF),
            pltpu.VMEM((D, E), BF),
            pltpu.VMEM((VIDS, NEG, COUNT), I32),
            pltpu.VMEM((COUNT, VIDS * NEG), F32),
            pltpu.VMEM((D, D), BF),
            pltpu.VMEM((PATCH, 160, D), BF),
            pltpu.VMEM((PATCH * 160, D), BF),
            pltpu.VMEM((PATCH * COUNT, D), BF),
            pltpu.VMEM((4, D, 640), BF),
            pltpu.VMEM((256, D), BF),
            pltpu.VMEM((256, D), BF),
            pltpu.VMEM((4, 64, 128), F32),
            pltpu.VMEM((4, 4, 64, 256), F32),
            pltpu.VMEM((4, 4, 64, 256), F32),
            pltpu.VMEM((4, 256, 256), BF),
            pltpu.VMEM((4, 256, 256), BF),
            pltpu.VMEM((COUNT, D), F32),
            pltpu.VMEM((2, 4, 128, 128), F32),
            pltpu.VMEM((VIDS, 16, HALF), BF),
            pltpu.VMEM((VIDS, 16, HALF), BF),
            pltpu.VMEM((2, 16, HALF), BF),
            pltpu.VMEM((COUNT, E), BF),
            pltpu.VMEM((COUNT, COUNT), F32),
            pltpu.VMEM((COUNT, COUNT), F32),
            pltpu.VMEM((VIDS, PART, 128), F32),
            pltpu.VMEM((VIDS, PART, 128), F32),
            dma((8,)), dma((6,)), dma, dma((2,)), dma((2,)), dma, dma, dma((2,)), dma((2,)), dma, dma, dma, dma,
        ],
        compiler_params=pltpu.CompilerParams(
            collective_id=0, has_side_effects=True, vmem_limit_bytes=60 * 1024 * 1024
        ),
    )(
        valid,
        tokens.reshape(COUNT * PATCH, D),
        norm_gain.reshape(1, D),
        w_qkv,
        w_out,
        w_proj,
        offsets,
        jnp.swapaxes(negatives, 1, 2),
    )
    emb, losses = pl.pallas_call(
        hand_over,
        out_shape=(
            jax.ShapeDtypeStruct((COUNT, E), BF),
            jax.ShapeDtypeStruct((1, COUNT), F32),
        ),
        in_specs=[vmem, vmem],
        out_specs=(vmem, vmem),
    )(emb, losses)
    return emb.reshape(1, COUNT, E), losses


def solution(mesh):
    placed = (
        P("vid", "tm", None, None),
        P(),
        P(),
        P(),
        P(),
        P("vid", "tm"),
        P(None, "tm", None),
        P(),
    )
    return jax.shard_map(
        local,
        mesh=mesh,
        in_specs=placed,
        out_specs=(P("vid", "tm", None), P("vid", "tm")),
        check_vma=False,
    )
```

```python
import itertools
import math

import jax
import jax.numpy as jnp
from jax import lax
from jax.experimental import pallas as pl
from jax.experimental.pallas import tpu as pltpu
from jax.sharding import PartitionSpec as P

MESH = pl.DeviceIdType.MESH
BF, F32, I32 = jnp.bfloat16, jnp.float32, jnp.int32
D = 1024
E = 2048
PATCH = 16
WINDOW = 16
REACH = 8
COUNT = 128
VIDS = 16
TMS = 8
NEG = 8
PART = COUNT // VIDS
HALF = D // 2


def nn(a, b):
    return lax.dot_general(a, b, (((1,), (0,)), ((), ())), preferred_element_type=F32)


def nt(a, b):
    return lax.dot_general(a, b, (((1,), (1,)), ((), ())), preferred_element_type=F32)


def iota(shape, dim):
    return lax.broadcasted_iota(I32, shape, dim)


def kernel(
    valid, tokens, gain, w_qkv, w_out, w_proj, offsets, negatives,
    emb_out, loss_out,
    perm, eye, avg, raw, halo, wq, wk, wv, wo, wp, negs, negt, wvt, xn, keys, queries, vt, y0, y1,
    bias, st0, st1, pr0, pr1, tokmean, acc, pack, got, near, own_e, count_out, count, lse_out, lse_in,
    tok_sem, w_sem, out_sem, halo_send, halo_recv, a_send, a_recv, n_send, n_recv, b_send, b_recv, c_send, c_recv,
):
    vid = lax.axis_index("vid")
    tm = lax.axis_index("tm")
    left = lax.rem(tm + TMS - 1, TMS)
    right = lax.rem(tm + 1, TMS)
    across = lax.rem(tm + TMS // 2, TMS)
    y_hi, z, core = vid // 8, vid // 2 % 4, vid % 2
    peers = [
        {"vid": (y_hi + dy) % 2 * 8 + (z + dz) % 4 * 2 + (core + dc) % 2, "tm": across}
        for dz in (2, 1, 3, 0) for dy in (1, 0) for dc in (1, 0)
    ]
    first = tm * COUNT
    length = valid[vid]

    tok_copies = [
        pltpu.make_async_copy(tokens.at[pl.ds(256 * b, 256)], raw.at[b], tok_sem.at[b])
        for b in range(8)
    ]
    w_copies = [
        pltpu.make_async_copy(src, dst, w_sem.at[i])
        for i, (src, dst) in enumerate(
            [
                (w_qkv.at[:, pl.ds(2 * D, D)], wv),
                (negatives, negs),
                (w_qkv.at[:, pl.ds(0, D)], wq),
                (w_qkv.at[:, pl.ds(D, D)], wk),
                (w_proj, wp),
            ]
        )
    ]
    out_copies = [
        pltpu.make_async_copy(
            w_out.at[pl.ds(256 * (2 * jp + j2) + 64 * h, 64)],
            wo.at[pl.ds(512 * jp + 128 * h + 64 * j2, 64)],
            w_sem.at[5],
        )
        for jp in range(2) for h in range(4) for j2 in range(2)
    ]
    barrier = pltpu.get_barrier_semaphore()
    for peer in peers:
        pl.semaphore_signal(barrier, inc=1, device_id=peer, device_id_type=MESH)
    for peer in (left, right):
        pl.semaphore_signal(barrier, inc=1, device_id={"tm": peer}, device_id_type=MESH)
    w_copies[1].start()
    tok_copies[0].start()
    w_copies[0].start()
    for copy in tok_copies[1:]:
        copy.start()

    r0, r1 = iota((256, 256), 0), iota((256, 256), 1)
    perm[...] = (r1 == (r0 % 16) * 16 + r0 // 16).astype(F32).astype(BF)
    eye[...] = (r0 == r1).astype(F32).astype(BF)
    avg[...] = jnp.where(iota((16, 256), 0) == iota((16, 256), 1) // 16, 1.0 / PATCH, 0.0).astype(BF)

    g0, f0 = iota((64, 128), 0), iota((64, 128), 1) % 32
    for b in range(4):
        frame = g0 + (32 * b - WINDOW)
        query = f0 + 32 * b
        glob = frame + first
        ok = (jnp.abs(frame - query) <= WINDOW) & (glob >= 0) & (glob < TMS * COUNT)
        ok = ok & ((glob < length) | (frame == query))
        bias[b] = jnp.where(ok, 0.0, -1e30)
    lane_block = iota((64, 128), 1) // 32

    w_copies[1].wait()
    lane = iota((COUNT, COUNT), 1)
    row = iota((COUNT, COUNT), 0)
    negt[...] = jnp.transpose(negs[...].reshape(VIDS * NEG, COUNT).astype(F32))
    ids = negt[pl.ds(pl.multiple_of(PART * vid, PART), PART), :]
    ids = jnp.concatenate([ids] * VIDS, axis=0)
    times = jnp.zeros((COUNT, COUNT), F32)
    for k in range(NEG):
        one = jnp.sum(jnp.where(lane == row // PART * NEG + k, ids, 0.0), axis=1, keepdims=True)
        times += (one * PART + (row % PART).astype(F32) == lane.astype(F32)).astype(F32)
    count_out[...] = times

    pl.semaphore_wait(barrier, VIDS + 2)

    halo_copies = [
        pltpu.make_async_remote_copy(
            src_ref=tokens.at[pl.ds(256 * 7, 256)], dst_ref=halo.at[0],
            send_sem=halo_send.at[0], recv_sem=halo_recv.at[0],
            device_id={"tm": right}, device_id_type=MESH,
        ),
        pltpu.make_async_remote_copy(
            src_ref=tokens.at[pl.ds(0, 256)], dst_ref=halo.at[1],
            send_sem=halo_send.at[1], recv_sem=halo_recv.at[1],
            device_id={"tm": left}, device_id_type=MESH,
        ),
    ]
    for copy in halo_copies:
        copy.start()

    count_copy = pltpu.make_async_remote_copy(
        src_ref=count_out, dst_ref=count, send_sem=c_send, recv_sem=c_recv, device_id=peers[-1], device_id_type=MESH,
    )
    count_copy.start()

    def normed(block, out, rows=(0, 1, 2, 3)):
        for c in rows:
            for n in range(4):
                at = 64 * c + 16 * n
                x = block[at:at + 16, :].astype(F32)
                mean = jnp.sum(x * x, axis=1, keepdims=True) * (1.0 / D)
                out[at:at + 16, :] = (x * lax.rsqrt(mean + 1e-5) * gain[...]).astype(BF)
            yield

    def permuted(y, rows):
        for c in range(4):
            part = nn(perm[...], y[:, 256 * c:256 * c + 256]).astype(BF)
            xn[:, rows, 256 * c:256 * c + 256] = part.reshape(PATCH, 16, 256)
            yield

    def averaged(b):
        tokmean[pl.ds(pl.multiple_of(16 * b, 16), 16), :] = nn(avg[...], raw[b])
        yield

    def rows_of(b):
        return pl.ds(pl.multiple_of(16 * b + 16, 16), 16)

    def flip(a):
        for c in range(4):
            block = nt(eye[...], wv[256 * c:256 * c + 256, pl.ds(a, 256)])
            wvt[pl.ds(a, 256), 256 * c:256 * c + 256] = block.astype(BF)
            yield

    def weave(*jobs):
        for _ in itertools.zip_longest(*jobs):
            pass

    def arrived(b):
        pltpu.make_async_copy(tokens.at[pl.ds(0, 256)], raw.at[b], tok_sem.at[b]).wait()

    arrived(0)
    weave(normed(raw.at[0], y0))
    w_copies[0].wait()
    w_copies[2].start()

    def norm_pair(i, carry):
        b = 2 * i
        arrived(b + 1)
        arrived(b + 2)
        weave(permuted(y0, rows_of(b)), normed(raw.at[b + 1], y1), averaged(b), flip(pl.multiple_of(256 * i, 256)))
        weave(permuted(y1, rows_of(b + 1)), normed(raw.at[b + 2], y0), averaged(b + 1))
        return carry

    lax.fori_loop(0, 3, norm_pair, 0)
    arrived(7)
    weave(permuted(y0, rows_of(6)), normed(raw.at[7], y1), averaged(6), flip(768))
    weave(permuted(y1, rows_of(7)), averaged(7))
    w_copies[3].start()

    w_copies[2].wait()
    scale = math.log2(math.e) / 8.0

    def project_queries(i, carry):
        rows = pl.ds(pl.multiple_of(512 * i, 512), 512)
        x = xn[pl.ds(4 * i, 4), 16:16 + COUNT, :].reshape(512, D)
        for c in range(2):
            queries[rows, 512 * c:512 * c + 512] = (nn(x, wq[:, 512 * c:512 * c + 512]) * scale).astype(BF)
        return carry

    lax.fori_loop(0, 4, project_queries, 0)

    for copy in w_copies[4:] + out_copies:
        copy.start()

    def values(ga, ra, gb, rb):
        xa = xn[pl.ds(4 * ga, 4), 32 * ra:32 * ra + 32, :].reshape(128, D)
        xb = xn[pl.ds(4 * gb, 4), 32 * rb:32 * rb + 32, :].reshape(128, D)
        x2 = jnp.concatenate([xa, xb], axis=0)
        for c in range(2):
            r = nt(wvt[512 * c:512 * c + 512], x2).astype(BF)
            vt[ga, 512 * c:512 * c + 512, 128 * ra:128 * ra + 128] = r[:, :128]
            vt[gb, 512 * c:512 * c + 512, 128 * rb:128 * rb + 128] = r[:, 128:]
            yield

    def values_inner(i, carry):
        weave(values(2 * i, 1, 2 * i, 2))
        weave(values(2 * i + 1, 1, 2 * i + 1, 2))
        return carry

    lax.fori_loop(0, 2, values_inner, 0)

    halo_copies[0].wait_recv()
    halo_copies[1].wait_recv()
    weave(values(0, 3, 1, 3), normed(halo.at[0], y0))
    weave(values(2, 3, 3, 3), normed(halo.at[1], y1))
    weave(permuted(y0, pl.ds(0, 16)), permuted(y1, pl.ds(16 + COUNT, 16)))

    w_copies[3].wait()

    def project_keys(i, carry):
        rows = pl.ds(pl.multiple_of(512 * i, 512), 512)
        for c in range(2):
            keys[rows, 512 * c:512 * c + 512] = nn(xn.reshape(PATCH * 160, D)[rows, :], wk[:, 512 * c:512 * c + 512]).astype(BF)
        return carry

    lax.fori_loop(0, 5, project_keys, 0)

    def values_outer(i, carry):
        weave(values(2 * i, 0, 2 * i, 4))
        weave(values(2 * i + 1, 0, 2 * i + 1, 4))
        return carry

    lax.fori_loop(0, 2, values_outer, 0)

    acc[...] = jnp.zeros_like(acc)

    def where_is(u):
        return u // 4, pl.ds(pl.multiple_of(256 * (u % 4), 256), 256)

    head_lanes = [iota((32, 256), 1) // 64 == h for h in range(4)]

    def diagonal(x):
        return [jnp.where(head_lanes[h], x, jnp.zeros_like(x)) for h in range(4)]

    def probs_of(u, out):
        g, cols = where_is(u)
        for q in range(4):
            for b in range(4):
                ps = [8 * g + 2 * q, 8 * g + 2 * q + 1]
                q2 = [queries[pl.ds(pl.multiple_of(COUNT * p + 32 * b, 32), 32), cols] for p in ps]
                k2 = [keys[pl.ds(pl.multiple_of(160 * p + 32 * b, 32), 64), cols] for p in ps]
                r = nt(jnp.concatenate(k2, axis=0), jnp.concatenate(diagonal(q2[0]) + diagonal(q2[1]), axis=0))
                for n in range(2):
                    s = r[64 * n:64 * n + 64, 128 * n:128 * n + 128] + bias[b]
                    e = jnp.exp2(s - jnp.max(s, axis=0, keepdims=True))
                    e = (e * (1.0 / jnp.sum(e, axis=0, keepdims=True))).astype(BF)
                    at = 256 * (q // 2) + 64 * (q % 2) + 32 * n
                    out[b, at:at + 32, :] = e[:32]
                    out[b, 128 + at:128 + at + 32, :] = e[32:]
                yield

    def attended_of(u, probs):
        g, rows = where_is(u)
        for b in range(4):
            lanes = slice(128 * b, 128 * b + 256)
            v = jnp.concatenate([vt[2 * g, rows, lanes], vt[2 * g + 1, rows, lanes]], axis=1)
            r = nn(v, probs[b])
            part = r[:64]
            for h in range(1, 4):
                part = jnp.where(lane_block == h, r[64 * h:64 * h + 64], part)
            acc[u % 4, b] += part
            for _ in range(4):
                yield

    weave(probs_of(0, pr0))

    def attend(i, carry):
        u = 2 * i
        weave(probs_of(u + 1, pr1), attended_of(u, pr0))
        weave(probs_of(u + 2, pr0), attended_of(u + 1, pr1))
        return carry

    lax.fori_loop(0, 3, attend, 0)
    weave(probs_of(7, pr1), attended_of(6, pr0))
    weave(attended_of(7, pr1))

    pltpu.make_async_copy(w_out, wo, w_sem.at[5]).wait()
    att = []
    for b in range(4):
        pairs = [jnp.concatenate([acc[2 * jp, b], acc[2 * jp + 1, b]], axis=0) for jp in range(2)]
        turned = [jnp.transpose(pair * (1.0 / PATCH)).astype(BF) for pair in pairs]
        att.append(jnp.concatenate([t[32 * h:32 * h + 32] for t in turned for h in range(4)], axis=1))
    pooled = tokmean[...] + nn(jnp.concatenate(att, axis=0), wo[...])
    blocks = pooled.reshape(VIDS, PART, D)
    pack[...] = jnp.concatenate([blocks[:, :, :HALF], blocks[:, :, HALF:]], axis=1).astype(BF)

    pooled_copies = [
        pltpu.make_async_remote_copy(
            src_ref=pack.at[peers[k]["vid"]], dst_ref=got.at[vid],
            send_sem=a_send, recv_sem=a_recv,
            device_id=peers[k], device_id_type=MESH,
        )
        for k in range(VIDS)
    ]
    near_copies = [
        pltpu.make_async_remote_copy(
            src_ref=pack.at[VIDS - 1], dst_ref=near.at[0],
            send_sem=n_send.at[0], recv_sem=n_recv.at[0],
            device_id={"tm": right}, device_id_type=MESH,
        ),
        pltpu.make_async_remote_copy(
            src_ref=pack.at[0], dst_ref=near.at[1],
            send_sem=n_send.at[1], recv_sem=n_recv.at[1],
            device_id={"tm": left}, device_id_type=MESH,
        ),
    ]
    for copy in pooled_copies + near_copies:
        copy.start()

    w_copies[4].wait()
    own_e[...] = nn(pooled.astype(BF), wp[...]).astype(BF)
    out_copy = pltpu.make_async_copy(own_e, emb_out, out_sem)
    out_copy.start()

    e = own_e[...]
    near_own = nt(e, e)

    for copy in near_copies:
        copy.wait_recv()
    pltpu.make_async_copy(got, got, a_recv).wait()
    seen = jnp.concatenate([got[...], near[...]], axis=0).astype(F32)
    seen = jnp.concatenate([seen[:, :PART], seen[:, PART:]], axis=2)
    seen = seen.reshape((VIDS + 2) * PART, D).astype(BF)
    all_e = nn(seen, wp[...]).astype(BF)
    factor = 8.0 / math.sqrt(E)
    gram = nt(all_e[:COUNT], all_e[:COUNT]) * factor

    frame_here = across * COUNT + PART * vid + lane % PART
    other = jnp.zeros((COUNT, COUNT), I32)
    for m in range(VIDS):
        other = jnp.where(lane // PART == m, valid[m], other)
    count_copy.wait_recv()
    times = count[...]
    neg = jnp.where(frame_here < other, gram, -1e30)
    top = jnp.max(jnp.where(times > 0, neg, -3e38), axis=1, keepdims=True)
    some = jnp.sum(jnp.where(times > 0, times * jnp.exp(jnp.minimum(neg - top, 0.0)), 0.0), axis=1, keepdims=True)
    lse = top + jnp.log(some)
    lse_out[...] = jnp.broadcast_to(lse, (COUNT, 128)).reshape(VIDS, PART, 128)

    back_copies = [
        pltpu.make_async_remote_copy(
            src_ref=lse_out.at[peers[k]["vid"]], dst_ref=lse_in.at[vid],
            send_sem=b_send, recv_sem=b_recv,
            device_id=peers[k], device_id_type=MESH,
        )
        for k in range(VIDS)
    ]
    for copy in back_copies:
        copy.start()

    near_e = nt(all_e[COUNT:], e)
    scores = jnp.concatenate([near_e[:REACH], near_own, near_e[REACH:]], axis=0)
    off = offsets[...]
    here = first + iota((1, COUNT), 1)
    ahead = here + off
    inside = (ahead >= 0) & (ahead < length)
    slot = jnp.where(inside, ahead, here - off) - first + REACH
    pick = iota((COUNT + 2 * REACH, COUNT), 0) == slot
    pos = jnp.sum(jnp.where(pick, scores, 0.0), axis=0, keepdims=True) * factor

    pltpu.make_async_copy(lse_in, lse_in, b_recv).wait()
    back = lse_in[...].reshape(COUNT, 128)
    lse_neg = jnp.sum(jnp.where(row == lane, back, 0.0), axis=0, keepdims=True)
    peak = jnp.maximum(pos, lse_neg)
    total = peak + jnp.log(jnp.exp(pos - peak) + jnp.exp(lse_neg - peak))
    loss_out[...] = jnp.where(here < length, total - pos, 0.0)

    for copy in halo_copies + near_copies + [count_copy]:
        copy.wait_send()
    pltpu.make_async_copy(pack, pack, a_send).wait()
    pltpu.make_async_copy(lse_out, lse_out, b_send).wait()
    out_copy.wait()


def hand_over(emb, losses, emb_out, loss_out):
    emb_out[...] = emb[...]
    loss_out[...] = losses[...]


def local(tokens, norm_gain, w_qkv, w_out, w_proj, offsets, negatives, valid):
    anywhere = pl.BlockSpec(memory_space=pl.ANY)
    vmem = pl.BlockSpec(memory_space=pltpu.VMEM)
    dma = pltpu.SemaphoreType.DMA
    emb, losses = pl.pallas_call(
        kernel,
        out_shape=(
            jax.ShapeDtypeStruct((COUNT, E), BF),
            jax.ShapeDtypeStruct((1, COUNT), F32),
        ),
        in_specs=[
            pl.BlockSpec(memory_space=pltpu.SMEM), anywhere, vmem, anywhere, anywhere, anywhere, vmem, anywhere,
        ],
        out_specs=(anywhere, vmem),
        scratch_shapes=[
            pltpu.VMEM((256, 256), BF),
            pltpu.VMEM((256, 256), BF),
            pltpu.VMEM((16, 256), BF),
            pltpu.VMEM((8, 256, D), BF),
            pltpu.VMEM((2, 256, D), BF),
            pltpu.VMEM((D, D), BF),
            pltpu.VMEM((D, D), BF),
            pltpu.VMEM((D, D), BF),
            pltpu.VMEM((D, D), BF),
            pltpu.VMEM((D, E), BF),
            pltpu.VMEM((VIDS, NEG, COUNT), I32),
            pltpu.VMEM((COUNT, VIDS * NEG), F32),
            pltpu.VMEM((D, D), BF),
            pltpu.VMEM((PATCH, 160, D), BF),
            pltpu.VMEM((PATCH * 160, D), BF),
            pltpu.VMEM((PATCH * COUNT, D), BF),
            pltpu.VMEM((4, D, 640), BF),
            pltpu.VMEM((256, D), BF),
            pltpu.VMEM((256, D), BF),
            pltpu.VMEM((4, 64, 128), F32),
            pltpu.VMEM((4, 4, 64, 256), F32),
            pltpu.VMEM((4, 4, 64, 256), F32),
            pltpu.VMEM((4, 512, 128), BF),
            pltpu.VMEM((4, 512, 128), BF),
            pltpu.VMEM((COUNT, D), F32),
            pltpu.VMEM((4, 4, 64, 128), F32),
            pltpu.VMEM((VIDS, 16, HALF), BF),
            pltpu.VMEM((VIDS, 16, HALF), BF),
            pltpu.VMEM((2, 16, HALF), BF),
            pltpu.VMEM((COUNT, E), BF),
            pltpu.VMEM((COUNT, COUNT), F32),
            pltpu.VMEM((COUNT, COUNT), F32),
            pltpu.VMEM((VIDS, PART, 128), F32),
            pltpu.VMEM((VIDS, PART, 128), F32),
            dma((8,)), dma((6,)), dma, dma((2,)), dma((2,)), dma, dma, dma((2,)), dma((2,)), dma, dma, dma, dma,
        ],
        compiler_params=pltpu.CompilerParams(
            collective_id=0, has_side_effects=True, vmem_limit_bytes=60 * 1024 * 1024
        ),
    )(
        valid,
        tokens.reshape(COUNT * PATCH, D),
        norm_gain.reshape(1, D),
        w_qkv,
        w_out,
        w_proj,
        offsets,
        jnp.swapaxes(negatives, 1, 2),
    )
    emb, losses = pl.pallas_call(
        hand_over,
        out_shape=(
            jax.ShapeDtypeStruct((COUNT, E), BF),
            jax.ShapeDtypeStruct((1, COUNT), F32),
        ),
        in_specs=[vmem, vmem],
        out_specs=(vmem, vmem),
    )(emb, losses)
    return emb.reshape(1, COUNT, E), losses


def solution(mesh):
    placed = (
        P("vid", "tm", None, None),
        P(),
        P(),
        P(),
        P(),
        P("vid", "tm"),
        P(None, "tm", None),
        P(),
    )
    return jax.shard_map(
        local,
        mesh=mesh,
        in_specs=placed,
        out_specs=(P("vid", "tm", None), P("vid", "tm")),
        check_vma=False,
    )
```

```python
import itertools
import math

import jax
import jax.numpy as jnp
from jax import lax
from jax.experimental import pallas as pl
from jax.experimental.pallas import tpu as pltpu
from jax.sharding import PartitionSpec as P

MESH = pl.DeviceIdType.MESH
BF, F32, I32 = jnp.bfloat16, jnp.float32, jnp.int32
D = 1024
E = 2048
PATCH = 16
WINDOW = 16
REACH = 8
COUNT = 128
VIDS = 16
TMS = 8
NEG = 8
PART = COUNT // VIDS
HALF = D // 2


def nn(a, b):
    return lax.dot_general(a, b, (((1,), (0,)), ((), ())), preferred_element_type=F32)


def nt(a, b):
    return lax.dot_general(a, b, (((1,), (1,)), ((), ())), preferred_element_type=F32)


def iota(shape, dim):
    return lax.broadcasted_iota(I32, shape, dim)


def kernel(
    valid, tokens, gain, w_qkv, w_out, w_proj, offsets, negatives,
    emb_out, loss_out,
    perm, eye, avg, raw, halo, wq, wk, wv, wo, wp, negs, negt, wvt, xn, keys, queries, vt, y0, y1,
    bias, st0, st1, pr0, pr1, tokmean, acc, pack, got, near, own_e, count_out, count, lse_out, lse_in,
    tok_sem, w_sem, out_sem, halo_send, halo_recv, a_send, a_recv, n_send, n_recv, b_send, b_recv, c_send, c_recv,
):
    vid = lax.axis_index("vid")
    tm = lax.axis_index("tm")
    left = lax.rem(tm + TMS - 1, TMS)
    right = lax.rem(tm + 1, TMS)
    across = lax.rem(tm + TMS // 2, TMS)
    y_hi, z, core = vid // 8, vid // 2 % 4, vid % 2
    peers = [
        {"vid": (y_hi + dy) % 2 * 8 + (z + dz) % 4 * 2 + (core + dc) % 2, "tm": across}
        for dz in (2, 1, 3, 0) for dy in (1, 0) for dc in (1, 0)
    ]
    first = tm * COUNT
    length = valid[vid]

    tok_copies = [
        pltpu.make_async_copy(tokens.at[pl.ds(256 * b, 256)], raw.at[b], tok_sem.at[b])
        for b in range(8)
    ]
    w_copies = [
        pltpu.make_async_copy(src, dst, w_sem.at[i])
        for i, (src, dst) in enumerate(
            [
                (w_qkv.at[:, pl.ds(2 * D, D)], wv),
                (negatives, negs),
                (w_qkv.at[:, pl.ds(0, D)], wq),
                (w_qkv.at[:, pl.ds(D, D)], wk),
                (w_proj, wp),
            ]
        )
    ]
    out_copies = [
        pltpu.make_async_copy(
            w_out.at[pl.ds(256 * (2 * jp + j2) + 64 * h, 64)],
            wo.at[pl.ds(512 * jp + 128 * h + 64 * j2, 64)],
            w_sem.at[5],
        )
        for jp in range(2) for h in range(4) for j2 in range(2)
    ]
    barrier = pltpu.get_barrier_semaphore()
    for peer in peers:
        pl.semaphore_signal(barrier, inc=1, device_id=peer, device_id_type=MESH)
    for peer in (left, right):
        pl.semaphore_signal(barrier, inc=1, device_id={"tm": peer}, device_id_type=MESH)
    w_copies[1].start()
    tok_copies[0].start()
    w_copies[0].start()
    for copy in tok_copies[1:]:
        copy.start()

    r0, r1 = iota((256, 256), 0), iota((256, 256), 1)
    perm[...] = (r1 == (r0 % 16) * 16 + r0 // 16).astype(F32).astype(BF)
    eye[...] = (r0 == r1).astype(F32).astype(BF)
    avg[...] = jnp.where(iota((16, 256), 0) == iota((16, 256), 1) // 16, 1.0 / PATCH, 0.0).astype(BF)

    g0, f0 = iota((64, 128), 0), iota((64, 128), 1) % 32
    for b in range(4):
        frame = g0 + (32 * b - WINDOW)
        query = f0 + 32 * b
        glob = frame + first
        ok = (jnp.abs(frame - query) <= WINDOW) & (glob >= 0) & (glob < TMS * COUNT)
        ok = ok & ((glob < length) | (frame == query))
        bias[b] = jnp.where(ok, 0.0, -1e30)
    lane_block = iota((64, 128), 1) // 32

    w_copies[1].wait()
    lane = iota((COUNT, COUNT), 1)
    row = iota((COUNT, COUNT), 0)
    negt[...] = jnp.transpose(negs[...].reshape(VIDS * NEG, COUNT).astype(F32))
    ids = negt[pl.ds(pl.multiple_of(PART * vid, PART), PART), :]
    ids = jnp.concatenate([ids] * VIDS, axis=0)
    times = jnp.zeros((COUNT, COUNT), F32)
    for k in range(NEG):
        one = jnp.sum(jnp.where(lane == row // PART * NEG + k, ids, 0.0), axis=1, keepdims=True)
        times += (one * PART + (row % PART).astype(F32) == lane.astype(F32)).astype(F32)
    count_out[...] = times

    pl.semaphore_wait(barrier, VIDS + 2)

    halo_copies = [
        pltpu.make_async_remote_copy(
            src_ref=tokens.at[pl.ds(256 * 7, 256)], dst_ref=halo.at[0],
            send_sem=halo_send.at[0], recv_sem=halo_recv.at[0],
            device_id={"tm": right}, device_id_type=MESH,
        ),
        pltpu.make_async_remote_copy(
            src_ref=tokens.at[pl.ds(0, 256)], dst_ref=halo.at[1],
            send_sem=halo_send.at[1], recv_sem=halo_recv.at[1],
            device_id={"tm": left}, device_id_type=MESH,
        ),
    ]
    for copy in halo_copies:
        copy.start()

    count_copy = pltpu.make_async_remote_copy(
        src_ref=count_out, dst_ref=count, send_sem=c_send, recv_sem=c_recv, device_id=peers[-1], device_id_type=MESH,
    )
    count_copy.start()

    def normed(block, out, rows=(0, 1, 2, 3)):
        for c in rows:
            for n in range(4):
                at = 64 * c + 16 * n
                x = block[at:at + 16, :].astype(F32)
                mean = jnp.sum(x * x, axis=1, keepdims=True) * (1.0 / D)
                out[at:at + 16, :] = (x * lax.rsqrt(mean + 1e-5) * gain[...]).astype(BF)
            yield

    def permuted(y, rows):
        for c in range(4):
            part = nn(perm[...], y[:, 256 * c:256 * c + 256]).astype(BF)
            xn[:, rows, 256 * c:256 * c + 256] = part.reshape(PATCH, 16, 256)
            yield

    def averaged(b):
        tokmean[pl.ds(pl.multiple_of(16 * b, 16), 16), :] = nn(avg[...], raw[b])
        yield

    def rows_of(b):
        return pl.ds(pl.multiple_of(16 * b + 16, 16), 16)

    def flip(a):
        for c in range(4):
            block = nt(eye[...], wv[256 * c:256 * c + 256, pl.ds(a, 256)])
            wvt[pl.ds(a, 256), 256 * c:256 * c + 256] = block.astype(BF)
            yield

    def weave(*jobs):
        for _ in itertools.zip_longest(*jobs):
            pass

    def arrived(b):
        pltpu.make_async_copy(tokens.at[pl.ds(0, 256)], raw.at[b], tok_sem.at[b]).wait()

    arrived(0)
    weave(normed(raw.at[0], y0))
    w_copies[0].wait()
    w_copies[2].start()

    def norm_pair(i, carry):
        b = 2 * i
        arrived(b + 1)
        arrived(b + 2)
        weave(permuted(y0, rows_of(b)), normed(raw.at[b + 1], y1), averaged(b), flip(pl.multiple_of(256 * i, 256)))
        weave(permuted(y1, rows_of(b + 1)), normed(raw.at[b + 2], y0), averaged(b + 1))
        return carry

    lax.fori_loop(0, 3, norm_pair, 0)
    arrived(7)
    weave(permuted(y0, rows_of(6)), normed(raw.at[7], y1), averaged(6), flip(768))
    weave(permuted(y1, rows_of(7)), averaged(7))
    w_copies[3].start()

    w_copies[2].wait()
    scale = math.log2(math.e) / 8.0

    def project_queries(i, carry):
        rows = pl.ds(pl.multiple_of(512 * i, 512), 512)
        x = xn[pl.ds(4 * i, 4), 16:16 + COUNT, :].reshape(512, D)
        for c in range(2):
            queries[rows, 512 * c:512 * c + 512] = (nn(x, wq[:, 512 * c:512 * c + 512]) * scale).astype(BF)
        return carry

    lax.fori_loop(0, 4, project_queries, 0)

    for copy in w_copies[4:] + out_copies:
        copy.start()

    def values(ga, ra, gb, rb):
        xa = xn[pl.ds(4 * ga, 4), 32 * ra:32 * ra + 32, :].reshape(128, D)
        xb = xn[pl.ds(4 * gb, 4), 32 * rb:32 * rb + 32, :].reshape(128, D)
        x2 = jnp.concatenate([xa, xb], axis=0)
        for c in range(2):
            r = nt(wvt[512 * c:512 * c + 512], x2).astype(BF)
            vt[ga, 512 * c:512 * c + 512, 128 * ra:128 * ra + 128] = r[:, :128]
            vt[gb, 512 * c:512 * c + 512, 128 * rb:128 * rb + 128] = r[:, 128:]
            yield

    def values_inner(i, carry):
        weave(values(2 * i, 1, 2 * i, 2))
        weave(values(2 * i + 1, 1, 2 * i + 1, 2))
        return carry

    lax.fori_loop(0, 2, values_inner, 0)

    weave(values(0, 3, 1, 3))
    weave(values(2, 3, 3, 3))

    w_copies[3].wait()

    def own_keys(i):
        x = xn[pl.ds(4 * i, 4), 16:16 + COUNT, :].reshape(512, D)
        for c in range(2):
            r = nn(x, wk[:, 512 * c:512 * c + 512]).astype(BF)
            keys[pl.ds(4 * i, 4), 16:16 + COUNT, 512 * c:512 * c + 512] = r.reshape(4, COUNT, 512)
            yield

    def project_keys(i, carry):
        weave(own_keys(i))
        return carry

    lax.fori_loop(0, 3, project_keys, 0)

    halo_copies[0].wait_recv()
    halo_copies[1].wait_recv()
    weave(own_keys(3), normed(halo.at[0], y0), normed(halo.at[1], y1))
    weave(permuted(y0, pl.ds(0, 16)), permuted(y1, pl.ds(16 + COUNT, 16)))
    x = jnp.concatenate([xn[:, :16, :], xn[:, 16 + COUNT:, :]], axis=1).reshape(512, D)
    for c in range(2):
        r = nn(x, wk[:, 512 * c:512 * c + 512]).astype(BF).reshape(PATCH, 32, 512)
        keys[:, :16, 512 * c:512 * c + 512] = r[:, :16]
        keys[:, 16 + COUNT:, 512 * c:512 * c + 512] = r[:, 16:]

    def values_outer(i, carry):
        weave(values(2 * i, 0, 2 * i, 4))
        weave(values(2 * i + 1, 0, 2 * i + 1, 4))
        return carry

    lax.fori_loop(0, 2, values_outer, 0)

    acc[...] = jnp.zeros_like(acc)

    def where_is(u):
        return u // 4, pl.ds(pl.multiple_of(256 * (u % 4), 256), 256)

    head_lanes = [iota((32, 256), 1) // 64 == h for h in range(4)]

    def diagonal(x):
        return [jnp.where(head_lanes[h], x, jnp.zeros_like(x)) for h in range(4)]

    def probs_of(u, out):
        g, cols = where_is(u)
        for q in range(4):
            for b in range(4):
                ps = [8 * g + 2 * q, 8 * g + 2 * q + 1]
                q2 = [queries[pl.ds(pl.multiple_of(COUNT * p + 32 * b, 32), 32), cols] for p in ps]
                k2 = [keys[p, 32 * b:32 * b + 64, cols] for p in ps]
                r = nt(jnp.concatenate(k2, axis=0), jnp.concatenate(diagonal(q2[0]) + diagonal(q2[1]), axis=0))
                for n in range(2):
                    s = r[64 * n:64 * n + 64, 128 * n:128 * n + 128] + bias[b]
                    e = jnp.exp2(s - jnp.max(s, axis=0, keepdims=True))
                    e = (e * (1.0 / jnp.sum(e, axis=0, keepdims=True))).astype(BF)
                    at = 256 * (q // 2) + 64 * (q % 2) + 32 * n
                    out[b, at:at + 32, :] = e[:32]
                    out[b, 128 + at:128 + at + 32, :] = e[32:]
                yield

    def attended_of(u, probs):
        g, rows = where_is(u)
        for b in range(4):
            lanes = slice(128 * b, 128 * b + 256)
            v = jnp.concatenate([vt[2 * g, rows, lanes], vt[2 * g + 1, rows, lanes]], axis=1)
            r = nn(v, probs[b])
            part = r[:64]
            for h in range(1, 4):
                part = jnp.where(lane_block == h, r[64 * h:64 * h + 64], part)
            acc[u % 4, b] += part
            for _ in range(4):
                yield

    weave(probs_of(0, pr0))

    def attend(i, carry):
        u = 2 * i
        weave(probs_of(u + 1, pr1), attended_of(u, pr0))
        weave(probs_of(u + 2, pr0), attended_of(u + 1, pr1))
        return carry

    lax.fori_loop(0, 3, attend, 0)
    weave(probs_of(7, pr1), attended_of(6, pr0))
    weave(attended_of(7, pr1))

    pltpu.make_async_copy(w_out, wo, w_sem.at[5]).wait()
    att = []
    for b in range(4):
        pairs = [jnp.concatenate([acc[2 * jp, b], acc[2 * jp + 1, b]], axis=0) for jp in range(2)]
        turned = [jnp.transpose(pair * (1.0 / PATCH)).astype(BF) for pair in pairs]
        att.append(jnp.concatenate([t[32 * h:32 * h + 32] for t in turned for h in range(4)], axis=1))
    pooled = tokmean[...] + nn(jnp.concatenate(att, axis=0), wo[...])
    blocks = pooled.reshape(VIDS, PART, D)
    pack[...] = jnp.concatenate([blocks[:, :, :HALF], blocks[:, :, HALF:]], axis=1).astype(BF)

    pooled_copies = [
        pltpu.make_async_remote_copy(
            src_ref=pack.at[peers[k]["vid"]], dst_ref=got.at[vid],
            send_sem=a_send, recv_sem=a_recv,
            device_id=peers[k], device_id_type=MESH,
        )
        for k in range(VIDS)
    ]
    near_copies = [
        pltpu.make_async_remote_copy(
            src_ref=pack.at[VIDS - 1], dst_ref=near.at[0],
            send_sem=n_send.at[0], recv_sem=n_recv.at[0],
            device_id={"tm": right}, device_id_type=MESH,
        ),
        pltpu.make_async_remote_copy(
            src_ref=pack.at[0], dst_ref=near.at[1],
            send_sem=n_send.at[1], recv_sem=n_recv.at[1],
            device_id={"tm": left}, device_id_type=MESH,
        ),
    ]
    for copy in pooled_copies + near_copies:
        copy.start()

    w_copies[4].wait()
    own_e[...] = nn(pooled.astype(BF), wp[...]).astype(BF)
    out_copy = pltpu.make_async_copy(own_e, emb_out, out_sem)
    out_copy.start()

    e = own_e[...]
    near_own = nt(e, e)

    for copy in near_copies:
        copy.wait_recv()
    pltpu.make_async_copy(got, got, a_recv).wait()
    seen = jnp.concatenate([got[...], near[...]], axis=0).astype(F32)
    seen = jnp.concatenate([seen[:, :PART], seen[:, PART:]], axis=2)
    seen = seen.reshape((VIDS + 2) * PART, D).astype(BF)
    all_e = nn(seen, wp[...]).astype(BF)
    factor = 8.0 / math.sqrt(E)
    gram = nt(all_e[:COUNT], all_e[:COUNT]) * factor

    frame_here = across * COUNT + PART * vid + lane % PART
    other = jnp.zeros((COUNT, COUNT), I32)
    for m in range(VIDS):
        other = jnp.where(lane // PART == m, valid[m], other)
    count_copy.wait_recv()
    times = count[...]
    neg = jnp.where(frame_here < other, gram, -1e30)
    top = jnp.max(jnp.where(times > 0, neg, -3e38), axis=1, keepdims=True)
    some = jnp.sum(jnp.where(times > 0, times * jnp.exp(jnp.minimum(neg - top, 0.0)), 0.0), axis=1, keepdims=True)
    lse = top + jnp.log(some)
    lse_out[...] = jnp.broadcast_to(lse, (COUNT, 128)).reshape(VIDS, PART, 128)

    back_copies = [
        pltpu.make_async_remote_copy(
            src_ref=lse_out.at[peers[k]["vid"]], dst_ref=lse_in.at[vid],
            send_sem=b_send, recv_sem=b_recv,
            device_id=peers[k], device_id_type=MESH,
        )
        for k in range(VIDS)
    ]
    for copy in back_copies:
        copy.start()

    near_e = nt(all_e[COUNT:], e)
    scores = jnp.concatenate([near_e[:REACH], near_own, near_e[REACH:]], axis=0)
    off = offsets[...]
    here = first + iota((1, COUNT), 1)
    ahead = here + off
    inside = (ahead >= 0) & (ahead < length)
    slot = jnp.where(inside, ahead, here - off) - first + REACH
    pick = iota((COUNT + 2 * REACH, COUNT), 0) == slot
    pos = jnp.sum(jnp.where(pick, scores, 0.0), axis=0, keepdims=True) * factor

    pltpu.make_async_copy(lse_in, lse_in, b_recv).wait()
    back = lse_in[...].reshape(COUNT, 128)
    lse_neg = jnp.sum(jnp.where(row == lane, back, 0.0), axis=0, keepdims=True)
    peak = jnp.maximum(pos, lse_neg)
    total = peak + jnp.log(jnp.exp(pos - peak) + jnp.exp(lse_neg - peak))
    loss_out[...] = jnp.where(here < length, total - pos, 0.0)

    for copy in halo_copies + near_copies + [count_copy]:
        copy.wait_send()
    pltpu.make_async_copy(pack, pack, a_send).wait()
    pltpu.make_async_copy(lse_out, lse_out, b_send).wait()
    out_copy.wait()


def hand_over(emb, losses, emb_out, loss_out):
    emb_out[...] = emb[...]
    loss_out[...] = losses[...]


def local(tokens, norm_gain, w_qkv, w_out, w_proj, offsets, negatives, valid):
    anywhere = pl.BlockSpec(memory_space=pl.ANY)
    vmem = pl.BlockSpec(memory_space=pltpu.VMEM)
    dma = pltpu.SemaphoreType.DMA
    emb, losses = pl.pallas_call(
        kernel,
        out_shape=(
            jax.ShapeDtypeStruct((COUNT, E), BF),
            jax.ShapeDtypeStruct((1, COUNT), F32),
        ),
        in_specs=[
            pl.BlockSpec(memory_space=pltpu.SMEM), anywhere, vmem, anywhere, anywhere, anywhere, vmem, anywhere,
        ],
        out_specs=(anywhere, vmem),
        scratch_shapes=[
            pltpu.VMEM((256, 256), BF),
            pltpu.VMEM((256, 256), BF),
            pltpu.VMEM((16, 256), BF),
            pltpu.VMEM((8, 256, D), BF),
            pltpu.VMEM((2, 256, D), BF),
            pltpu.VMEM((D, D), BF),
            pltpu.VMEM((D, D), BF),
            pltpu.VMEM((D, D), BF),
            pltpu.VMEM((D, D), BF),
            pltpu.VMEM((D, E), BF),
            pltpu.VMEM((VIDS, NEG, COUNT), I32),
            pltpu.VMEM((COUNT, VIDS * NEG), F32),
            pltpu.VMEM((D, D), BF),
            pltpu.VMEM((PATCH, 160, D), BF),
            pltpu.VMEM((PATCH, 160, D), BF),
            pltpu.VMEM((PATCH * COUNT, D), BF),
            pltpu.VMEM((4, D, 640), BF),
            pltpu.VMEM((256, D), BF),
            pltpu.VMEM((256, D), BF),
            pltpu.VMEM((4, 64, 128), F32),
            pltpu.VMEM((4, 4, 64, 256), F32),
            pltpu.VMEM((4, 4, 64, 256), F32),
            pltpu.VMEM((4, 512, 128), BF),
            pltpu.VMEM((4, 512, 128), BF),
            pltpu.VMEM((COUNT, D), F32),
            pltpu.VMEM((4, 4, 64, 128), F32),
            pltpu.VMEM((VIDS, 16, HALF), BF),
            pltpu.VMEM((VIDS, 16, HALF), BF),
            pltpu.VMEM((2, 16, HALF), BF),
            pltpu.VMEM((COUNT, E), BF),
            pltpu.VMEM((COUNT, COUNT), F32),
            pltpu.VMEM((COUNT, COUNT), F32),
            pltpu.VMEM((VIDS, PART, 128), F32),
            pltpu.VMEM((VIDS, PART, 128), F32),
            dma((8,)), dma((6,)), dma, dma((2,)), dma((2,)), dma, dma, dma((2,)), dma((2,)), dma, dma, dma, dma,
        ],
        compiler_params=pltpu.CompilerParams(
            collective_id=0, has_side_effects=True, vmem_limit_bytes=60 * 1024 * 1024
        ),
    )(
        valid,
        tokens.reshape(COUNT * PATCH, D),
        norm_gain.reshape(1, D),
        w_qkv,
        w_out,
        w_proj,
        offsets,
        jnp.swapaxes(negatives, 1, 2),
    )
    emb, losses = pl.pallas_call(
        hand_over,
        out_shape=(
            jax.ShapeDtypeStruct((COUNT, E), BF),
            jax.ShapeDtypeStruct((1, COUNT), F32),
        ),
        in_specs=[vmem, vmem],
        out_specs=(vmem, vmem),
    )(emb, losses)
    return emb.reshape(1, COUNT, E), losses


def solution(mesh):
    placed = (
        P("vid", "tm", None, None),
        P(),
        P(),
        P(),
        P(),
        P("vid", "tm"),
        P(None, "tm", None),
        P(),
    )
    return jax.shard_map(
        local,
        mesh=mesh,
        in_specs=placed,
        out_specs=(P("vid", "tm", None), P("vid", "tm")),
        check_vma=False,
    )
```

```python
import itertools
import math

import jax
import jax.numpy as jnp
from jax import lax
from jax.experimental import pallas as pl
from jax.experimental.pallas import tpu as pltpu
from jax.sharding import PartitionSpec as P

MESH = pl.DeviceIdType.MESH
BF, F32, I32 = jnp.bfloat16, jnp.float32, jnp.int32
D = 1024
E = 2048
PATCH = 16
WINDOW = 16
REACH = 8
COUNT = 128
VIDS = 16
TMS = 8
NEG = 8
PART = COUNT // VIDS
HALF = D // 2


def nn(a, b):
    return lax.dot_general(a, b, (((1,), (0,)), ((), ())), preferred_element_type=F32)


def nt(a, b):
    return lax.dot_general(a, b, (((1,), (1,)), ((), ())), preferred_element_type=F32)


def iota(shape, dim):
    return lax.broadcasted_iota(I32, shape, dim)


def kernel(
    valid, tokens, gain, w_qkv, w_out, w_proj, offsets, negatives,
    emb_out, loss_out,
    perm, eye, avg, raw, halo, wq, wk, wv, wo, wp, negs, negt, wvt, xn, keys, queries, vt, y0, y1,
    bias, st0, st1, pr0, pr1, tokmean, acc, pack, got, near, own_e, count_out, count, lse_out, lse_in,
    tok_sem, w_sem, out_sem, halo_send, halo_recv, a_send, a_recv, n_send, n_recv, b_send, b_recv, c_send, c_recv,
):
    vid = lax.axis_index("vid")
    tm = lax.axis_index("tm")
    left = lax.rem(tm + TMS - 1, TMS)
    right = lax.rem(tm + 1, TMS)
    across = lax.rem(tm + TMS // 2, TMS)
    y_hi, z, core = vid // 8, vid // 2 % 4, vid % 2
    peers = [
        {"vid": (y_hi + dy) % 2 * 8 + (z + dz) % 4 * 2 + (core + dc) % 2, "tm": across}
        for dz in (2, 1, 3, 0) for dy in (1, 0) for dc in (1, 0)
    ]
    first = tm * COUNT
    length = valid[vid]

    tok_copies = [
        pltpu.make_async_copy(tokens.at[pl.ds(256 * b, 256)], raw.at[b], tok_sem.at[b])
        for b in range(8)
    ]
    w_copies = [
        pltpu.make_async_copy(src, dst, w_sem.at[i])
        for i, (src, dst) in enumerate(
            [
                (w_qkv.at[:, pl.ds(2 * D, D)], wv),
                (negatives, negs),
                (w_qkv.at[:, pl.ds(0, D)], wq),
                (w_qkv.at[:, pl.ds(D, D)], wk),
                (w_proj, wp),
            ]
        )
    ]
    out_copies = [
        pltpu.make_async_copy(
            w_out.at[pl.ds(256 * (2 * jp + j2) + 64 * h, 64)],
            wo.at[pl.ds(512 * jp + 128 * h + 64 * j2, 64)],
            w_sem.at[5],
        )
        for jp in range(2) for h in range(4) for j2 in range(2)
    ]
    barrier = pltpu.get_barrier_semaphore()
    for peer in peers:
        pl.semaphore_signal(barrier, inc=1, device_id=peer, device_id_type=MESH)
    for peer in (left, right):
        pl.semaphore_signal(barrier, inc=1, device_id={"tm": peer}, device_id_type=MESH)
    w_copies[1].start()
    tok_copies[0].start()
    for copy in tok_copies[1:]:
        copy.start()

    r0, r1 = iota((256, 256), 0), iota((256, 256), 1)
    perm[...] = (r1 == (r0 % 16) * 16 + r0 // 16).astype(F32).astype(BF)
    eye[...] = (r0 == r1).astype(F32).astype(BF)
    avg[...] = jnp.where(iota((16, 256), 0) == iota((16, 256), 1) // 16, 1.0 / PATCH, 0.0).astype(BF)

    g0, f0 = iota((64, 128), 0), iota((64, 128), 1) % 32
    for b in range(4):
        frame = g0 + (32 * b - WINDOW)
        query = f0 + 32 * b
        glob = frame + first
        ok = (jnp.abs(frame - query) <= WINDOW) & (glob >= 0) & (glob < TMS * COUNT)
        ok = ok & ((glob < length) | (frame == query))
        bias[b] = jnp.where(ok, 0.0, -1e30)
    lane_block = iota((64, 128), 1) // 32

    w_copies[1].wait()
    lane = iota((COUNT, COUNT), 1)
    row = iota((COUNT, COUNT), 0)
    negt[...] = jnp.transpose(negs[...].reshape(VIDS * NEG, COUNT).astype(F32))
    ids = negt[pl.ds(pl.multiple_of(PART * vid, PART), PART), :]
    ids = jnp.concatenate([ids] * VIDS, axis=0)
    times = jnp.zeros((COUNT, COUNT), F32)
    for k in range(NEG):
        one = jnp.sum(jnp.where(lane == row // PART * NEG + k, ids, 0.0), axis=1, keepdims=True)
        times += (one * PART + (row % PART).astype(F32) == lane.astype(F32)).astype(F32)
    count_out[...] = times

    pl.semaphore_wait(barrier, VIDS + 2)

    halo_copies = [
        pltpu.make_async_remote_copy(
            src_ref=tokens.at[pl.ds(256 * 7, 256)], dst_ref=halo.at[0],
            send_sem=halo_send.at[0], recv_sem=halo_recv.at[0],
            device_id={"tm": right}, device_id_type=MESH,
        ),
        pltpu.make_async_remote_copy(
            src_ref=tokens.at[pl.ds(0, 256)], dst_ref=halo.at[1],
            send_sem=halo_send.at[1], recv_sem=halo_recv.at[1],
            device_id={"tm": left}, device_id_type=MESH,
        ),
    ]
    for copy in halo_copies:
        copy.start()

    count_copy = pltpu.make_async_remote_copy(
        src_ref=count_out, dst_ref=count, send_sem=c_send, recv_sem=c_recv, device_id=peers[-1], device_id_type=MESH,
    )
    count_copy.start()

    def normed(block, out, rows=(0, 1, 2, 3)):
        for c in rows:
            for n in range(4):
                at = 64 * c + 16 * n
                x = block[at:at + 16, :].astype(F32)
                mean = jnp.sum(x * x, axis=1, keepdims=True) * (1.0 / D)
                out[at:at + 16, :] = (x * lax.rsqrt(mean + 1e-5) * gain[...]).astype(BF)
            yield

    def permuted(y, rows):
        for c in range(4):
            part = nn(perm[...], y[:, 256 * c:256 * c + 256]).astype(BF)
            xn[:, rows, 256 * c:256 * c + 256] = part.reshape(PATCH, 16, 256)
            yield

    def averaged(b):
        tokmean[pl.ds(pl.multiple_of(16 * b, 16), 16), :] = nn(avg[...], raw[b])
        yield

    def rows_of(b):
        return pl.ds(pl.multiple_of(16 * b + 16, 16), 16)

    def flip(a):
        for c in range(4):
            wvt[pl.ds(a, 256), 256 * c:256 * c + 256] = jnp.transpose(wv[256 * c:256 * c + 256, pl.ds(a, 256)])
            yield

    def weave(*jobs):
        for _ in itertools.zip_longest(*jobs):
            pass

    def arrived(b):
        pltpu.make_async_copy(tokens.at[pl.ds(0, 256)], raw.at[b], tok_sem.at[b]).wait()

    arrived(0)
    weave(normed(raw.at[0], y0))
    w_copies[2].start()
    w_copies[0].start()

    def norm_pair(i, carry):
        b = 2 * i
        arrived(b + 1)
        arrived(b + 2)
        weave(permuted(y0, rows_of(b)), normed(raw.at[b + 1], y1), averaged(b))
        weave(permuted(y1, rows_of(b + 1)), normed(raw.at[b + 2], y0), averaged(b + 1))
        return carry

    lax.fori_loop(0, 3, norm_pair, 0)
    arrived(7)
    weave(permuted(y0, rows_of(6)), normed(raw.at[7], y1), averaged(6))
    weave(permuted(y1, rows_of(7)), averaged(7))
    w_copies[3].start()

    w_copies[0].wait()
    w_copies[2].wait()
    scale = math.log2(math.e) / 8.0

    def own_queries(i):
        rows = pl.ds(pl.multiple_of(512 * i, 512), 512)
        x = xn[pl.ds(4 * i, 4), 16:16 + COUNT, :].reshape(512, D)
        for c in range(2):
            queries[rows, 512 * c:512 * c + 512] = (nn(x, wq[:, 512 * c:512 * c + 512]) * scale).astype(BF)
            yield

    def project_queries(i, carry):
        weave(own_queries(i), flip(pl.multiple_of(256 * i, 256)))
        return carry

    lax.fori_loop(0, 4, project_queries, 0)

    for copy in w_copies[4:] + out_copies:
        copy.start()

    def values(ga, ra, gb, rb):
        xa = xn[pl.ds(4 * ga, 4), 32 * ra:32 * ra + 32, :].reshape(128, D)
        xb = xn[pl.ds(4 * gb, 4), 32 * rb:32 * rb + 32, :].reshape(128, D)
        x2 = jnp.concatenate([xa, xb], axis=0)
        for c in range(2):
            r = nt(wvt[512 * c:512 * c + 512], x2).astype(BF)
            vt[ga, 512 * c:512 * c + 512, 128 * ra:128 * ra + 128] = r[:, :128]
            vt[gb, 512 * c:512 * c + 512, 128 * rb:128 * rb + 128] = r[:, 128:]
            yield

    def values_inner(i, carry):
        weave(values(2 * i, 1, 2 * i, 2))
        weave(values(2 * i + 1, 1, 2 * i + 1, 2))
        return carry

    lax.fori_loop(0, 2, values_inner, 0)

    weave(values(0, 3, 1, 3))
    weave(values(2, 3, 3, 3))

    w_copies[3].wait()

    def own_keys(i):
        x = xn[pl.ds(4 * i, 4), 16:16 + COUNT, :].reshape(512, D)
        for c in range(2):
            r = nn(x, wk[:, 512 * c:512 * c + 512]).astype(BF)
            keys[pl.ds(4 * i, 4), 16:16 + COUNT, 512 * c:512 * c + 512] = r.reshape(4, COUNT, 512)
            yield

    def project_keys(i, carry):
        weave(own_keys(i))
        return carry

    lax.fori_loop(0, 3, project_keys, 0)

    halo_copies[0].wait_recv()
    halo_copies[1].wait_recv()
    weave(own_keys(3), normed(halo.at[0], y0), normed(halo.at[1], y1))
    weave(permuted(y0, pl.ds(0, 16)), permuted(y1, pl.ds(16 + COUNT, 16)))
    x = jnp.concatenate([xn[:, :16, :], xn[:, 16 + COUNT:, :]], axis=1).reshape(512, D)
    for c in range(2):
        r = nn(x, wk[:, 512 * c:512 * c + 512]).astype(BF).reshape(PATCH, 32, 512)
        keys[:, :16, 512 * c:512 * c + 512] = r[:, :16]
        keys[:, 16 + COUNT:, 512 * c:512 * c + 512] = r[:, 16:]

    def values_outer(i, carry):
        weave(values(2 * i, 0, 2 * i, 4))
        weave(values(2 * i + 1, 0, 2 * i + 1, 4))
        return carry

    lax.fori_loop(0, 2, values_outer, 0)

    acc[...] = jnp.zeros_like(acc)

    def where_is(u):
        return u // 4, pl.ds(pl.multiple_of(256 * (u % 4), 256), 256)

    head_lanes = [iota((32, 256), 1) // 64 == h for h in range(4)]

    def diagonal(x):
        return [jnp.where(head_lanes[h], x, jnp.zeros_like(x)) for h in range(4)]

    def probs_of(u, out):
        g, cols = where_is(u)
        for q in range(4):
            for b in range(4):
                ps = [8 * g + 2 * q, 8 * g + 2 * q + 1]
                q2 = [queries[pl.ds(pl.multiple_of(COUNT * p + 32 * b, 32), 32), cols] for p in ps]
                k2 = [keys[p, 32 * b:32 * b + 64, cols] for p in ps]
                r = nt(jnp.concatenate(k2, axis=0), jnp.concatenate(diagonal(q2[0]) + diagonal(q2[1]), axis=0))
                for n in range(2):
                    s = r[64 * n:64 * n + 64, 128 * n:128 * n + 128] + bias[b]
                    e = jnp.exp2(s - jnp.max(s, axis=0, keepdims=True))
                    e = (e * (1.0 / jnp.sum(e, axis=0, keepdims=True))).astype(BF)
                    at = 256 * (q // 2) + 64 * (q % 2) + 32 * n
                    out[b, at:at + 32, :] = e[:32]
                    out[b, 128 + at:128 + at + 32, :] = e[32:]
                yield

    def attended_of(u, probs):
        g, rows = where_is(u)
        for b in range(4):
            lanes = slice(128 * b, 128 * b + 256)
            v = jnp.concatenate([vt[2 * g, rows, lanes], vt[2 * g + 1, rows, lanes]], axis=1)
            r = nn(v, probs[b])
            part = r[:64]
            for h in range(1, 4):
                part = jnp.where(lane_block == h, r[64 * h:64 * h + 64], part)
            acc[u % 4, b] += part
            for _ in range(4):
                yield

    weave(probs_of(0, pr0))

    def attend(i, carry):
        u = 2 * i
        weave(probs_of(u + 1, pr1), attended_of(u, pr0))
        weave(probs_of(u + 2, pr0), attended_of(u + 1, pr1))
        return carry

    lax.fori_loop(0, 3, attend, 0)
    def project_out(jp):
        att = []
        for b in range(4):
            pair = jnp.concatenate([acc[2 * jp, b], acc[2 * jp + 1, b]], axis=0)
            turned = jnp.transpose(pair * (1.0 / PATCH)).astype(BF)
            att.append(jnp.concatenate([turned[32 * h:32 * h + 32] for h in range(4)], axis=1))
            yield
        att = jnp.concatenate(att, axis=0)
        for c in range(2):
            tokmean[:, 512 * c:512 * c + 512] += nn(att, wo[512 * jp:512 * jp + 512, 512 * c:512 * c + 512])
            yield

    pltpu.make_async_copy(w_out, wo, w_sem.at[5]).wait()
    weave(probs_of(7, pr1), attended_of(6, pr0), project_out(0))
    weave(attended_of(7, pr1))
    weave(project_out(1))

    pooled = tokmean[...]
    blocks = pooled.reshape(VIDS, PART, D)
    pack[...] = jnp.concatenate([blocks[:, :, :HALF], blocks[:, :, HALF:]], axis=1).astype(BF)

    pooled_copies = [
        pltpu.make_async_remote_copy(
            src_ref=pack.at[peers[k]["vid"]], dst_ref=got.at[vid],
            send_sem=a_send, recv_sem=a_recv,
            device_id=peers[k], device_id_type=MESH,
        )
        for k in range(VIDS)
    ]
    near_copies = [
        pltpu.make_async_remote_copy(
            src_ref=pack.at[VIDS - 1], dst_ref=near.at[0],
            send_sem=n_send.at[0], recv_sem=n_recv.at[0],
            device_id={"tm": right}, device_id_type=MESH,
        ),
        pltpu.make_async_remote_copy(
            src_ref=pack.at[0], dst_ref=near.at[1],
            send_sem=n_send.at[1], recv_sem=n_recv.at[1],
            device_id={"tm": left}, device_id_type=MESH,
        ),
    ]
    for copy in pooled_copies + near_copies:
        copy.start()

    w_copies[4].wait()
    own_e[...] = nn(pooled.astype(BF), wp[...]).astype(BF)
    out_copy = pltpu.make_async_copy(own_e, emb_out, out_sem)
    out_copy.start()

    e = own_e[...]
    near_own = nt(e, e)

    for copy in near_copies:
        copy.wait_recv()
    pltpu.make_async_copy(got, got, a_recv).wait()
    seen = jnp.concatenate([got[...], near[...]], axis=0).astype(F32)
    seen = jnp.concatenate([seen[:, :PART], seen[:, PART:]], axis=2)
    seen = seen.reshape((VIDS + 2) * PART, D).astype(BF)
    all_e = nn(seen, wp[...]).astype(BF)
    factor = 8.0 / math.sqrt(E)
    gram = nt(all_e[:COUNT], all_e[:COUNT]) * factor

    frame_here = across * COUNT + PART * vid + lane % PART
    other = jnp.zeros((COUNT, COUNT), I32)
    for m in range(VIDS):
        other = jnp.where(lane // PART == m, valid[m], other)
    count_copy.wait_recv()
    times = count[...]
    neg = jnp.where(frame_here < other, gram, -1e30)
    top = jnp.max(jnp.where(times > 0, neg, -3e38), axis=1, keepdims=True)
    some = jnp.sum(jnp.where(times > 0, times * jnp.exp(jnp.minimum(neg - top, 0.0)), 0.0), axis=1, keepdims=True)
    lse = top + jnp.log(some)
    lse_out[...] = jnp.broadcast_to(lse, (COUNT, 128)).reshape(VIDS, PART, 128)

    back_copies = [
        pltpu.make_async_remote_copy(
            src_ref=lse_out.at[peers[k]["vid"]], dst_ref=lse_in.at[vid],
            send_sem=b_send, recv_sem=b_recv,
            device_id=peers[k], device_id_type=MESH,
        )
        for k in range(VIDS)
    ]
    for copy in back_copies:
        copy.start()

    near_e = nt(all_e[COUNT:], e)
    scores = jnp.concatenate([near_e[:REACH], near_own, near_e[REACH:]], axis=0)
    off = offsets[...]
    here = first + iota((1, COUNT), 1)
    ahead = here + off
    inside = (ahead >= 0) & (ahead < length)
    slot = jnp.where(inside, ahead, here - off) - first + REACH
    pick = iota((COUNT + 2 * REACH, COUNT), 0) == slot
    pos = jnp.sum(jnp.where(pick, scores, 0.0), axis=0, keepdims=True) * factor

    pltpu.make_async_copy(lse_in, lse_in, b_recv).wait()
    back = lse_in[...].reshape(COUNT, 128)
    lse_neg = jnp.sum(jnp.where(row == lane, back, 0.0), axis=0, keepdims=True)
    peak = jnp.maximum(pos, lse_neg)
    total = peak + jnp.log(jnp.exp(pos - peak) + jnp.exp(lse_neg - peak))
    loss_out[...] = jnp.where(here < length, total - pos, 0.0)

    for copy in halo_copies + near_copies + [count_copy]:
        copy.wait_send()
    pltpu.make_async_copy(pack, pack, a_send).wait()
    pltpu.make_async_copy(lse_out, lse_out, b_send).wait()
    out_copy.wait()


def hand_over(emb, losses, emb_out, loss_out):
    emb_out[...] = emb[...]
    loss_out[...] = losses[...]


def local(tokens, norm_gain, w_qkv, w_out, w_proj, offsets, negatives, valid):
    anywhere = pl.BlockSpec(memory_space=pl.ANY)
    vmem = pl.BlockSpec(memory_space=pltpu.VMEM)
    dma = pltpu.SemaphoreType.DMA
    emb, losses = pl.pallas_call(
        kernel,
        out_shape=(
            jax.ShapeDtypeStruct((COUNT, E), BF),
            jax.ShapeDtypeStruct((1, COUNT), F32),
        ),
        in_specs=[
            pl.BlockSpec(memory_space=pltpu.SMEM), anywhere, vmem, anywhere, anywhere, anywhere, vmem, anywhere,
        ],
        out_specs=(anywhere, vmem),
        scratch_shapes=[
            pltpu.VMEM((256, 256), BF),
            pltpu.VMEM((256, 256), BF),
            pltpu.VMEM((16, 256), BF),
            pltpu.VMEM((8, 256, D), BF),
            pltpu.VMEM((2, 256, D), BF),
            pltpu.VMEM((D, D), BF),
            pltpu.VMEM((D, D), BF),
            pltpu.VMEM((D, D), BF),
            pltpu.VMEM((D, D), BF),
            pltpu.VMEM((D, E), BF),
            pltpu.VMEM((VIDS, NEG, COUNT), I32),
            pltpu.VMEM((COUNT, VIDS * NEG), F32),
            pltpu.VMEM((D, D), BF),
            pltpu.VMEM((PATCH, 160, D), BF),
            pltpu.VMEM((PATCH, 160, D), BF),
            pltpu.VMEM((PATCH * COUNT, D), BF),
            pltpu.VMEM((4, D, 640), BF),
            pltpu.VMEM((256, D), BF),
            pltpu.VMEM((256, D), BF),
            pltpu.VMEM((4, 64, 128), F32),
            pltpu.VMEM((4, 4, 64, 256), F32),
            pltpu.VMEM((4, 4, 64, 256), F32),
            pltpu.VMEM((4, 512, 128), BF),
            pltpu.VMEM((4, 512, 128), BF),
            pltpu.VMEM((COUNT, D), F32),
            pltpu.VMEM((4, 4, 64, 128), F32),
            pltpu.VMEM((VIDS, 16, HALF), BF),
            pltpu.VMEM((VIDS, 16, HALF), BF),
            pltpu.VMEM((2, 16, HALF), BF),
            pltpu.VMEM((COUNT, E), BF),
            pltpu.VMEM((COUNT, COUNT), F32),
            pltpu.VMEM((COUNT, COUNT), F32),
            pltpu.VMEM((VIDS, PART, 128), F32),
            pltpu.VMEM((VIDS, PART, 128), F32),
            dma((8,)), dma((6,)), dma, dma((2,)), dma((2,)), dma, dma, dma((2,)), dma((2,)), dma, dma, dma, dma,
        ],
        compiler_params=pltpu.CompilerParams(
            collective_id=0, has_side_effects=True, vmem_limit_bytes=60 * 1024 * 1024
        ),
    )(
        valid,
        tokens.reshape(COUNT * PATCH, D),
        norm_gain.reshape(1, D),
        w_qkv,
        w_out,
        w_proj,
        offsets,
        jnp.swapaxes(negatives, 1, 2),
    )
    emb, losses = pl.pallas_call(
        hand_over,
        out_shape=(
            jax.ShapeDtypeStruct((COUNT, E), BF),
            jax.ShapeDtypeStruct((1, COUNT), F32),
        ),
        in_specs=[vmem, vmem],
        out_specs=(vmem, vmem),
    )(emb, losses)
    return emb.reshape(1, COUNT, E), losses


def solution(mesh):
    placed = (
        P("vid", "tm", None, None),
        P(),
        P(),
        P(),
        P(),
        P("vid", "tm"),
        P(None, "tm", None),
        P(),
    )
    return jax.shard_map(
        local,
        mesh=mesh,
        in_specs=placed,
        out_specs=(P("vid", "tm", None), P("vid", "tm")),
        check_vma=False,
    )
```

```python
import itertools
import math

import jax
import jax.numpy as jnp
from jax import lax
from jax.experimental import pallas as pl
from jax.experimental.pallas import tpu as pltpu
from jax.sharding import PartitionSpec as P

MESH = pl.DeviceIdType.MESH
BF, F32, I32 = jnp.bfloat16, jnp.float32, jnp.int32
D = 1024
E = 2048
PATCH = 16
WINDOW = 16
REACH = 8
COUNT = 128
VIDS = 16
TMS = 8
NEG = 8
PART = COUNT // VIDS
HALF = D // 2


def nn(a, b):
    return lax.dot_general(a, b, (((1,), (0,)), ((), ())), preferred_element_type=F32)


def nt(a, b):
    return lax.dot_general(a, b, (((1,), (1,)), ((), ())), preferred_element_type=F32)


def iota(shape, dim):
    return lax.broadcasted_iota(I32, shape, dim)


def kernel(
    valid, tokens, gain, w_qkv, w_out, w_proj, offsets, negatives,
    emb_out, loss_out,
    perm, eye, avg, raw, halo, wq, wk, wv, wo, wp, negs, negt, wvt, xn, keys, queries, vt, y0, y1,
    bias, st0, st1, pr0, pr1, tokmean, acc, pack, got, near, own_e, count_out, count, lse_out, lse_in,
    tok_sem, w_sem, out_sem, halo_send, halo_recv, a_send, a_recv, n_send, n_recv, b_send, b_recv, c_send, c_recv,
):
    vid = lax.axis_index("vid")
    tm = lax.axis_index("tm")
    left = lax.rem(tm + TMS - 1, TMS)
    right = lax.rem(tm + 1, TMS)
    across = lax.rem(tm + TMS // 2, TMS)
    y_hi, z, core = vid // 8, vid // 2 % 4, vid % 2
    peers = [
        {"vid": (y_hi + dy) % 2 * 8 + (z + dz) % 4 * 2 + (core + dc) % 2, "tm": across}
        for dz in (2, 1, 3, 0) for dy in (1, 0) for dc in (1, 0)
    ]
    first = tm * COUNT
    length = valid[vid]

    tok_copies = [
        pltpu.make_async_copy(tokens.at[pl.ds(256 * b, 256)], raw.at[b], tok_sem.at[b])
        for b in range(8)
    ]
    w_copies = [
        pltpu.make_async_copy(src, dst, w_sem.at[i])
        for i, (src, dst) in enumerate(
            [
                (w_qkv.at[:, pl.ds(2 * D, D)], wv),
                (negatives, negs),
                (w_qkv.at[:, pl.ds(0, D)], wq),
                (w_qkv.at[:, pl.ds(D, D)], wk),
                (w_proj, wp),
            ]
        )
    ]
    w_copies[1].start()
    tok_copies[0].start()
    for copy in tok_copies[1:]:
        copy.start()
    out_copies = [
        pltpu.make_async_copy(w_out.at[jp, j2], wo.at[jp, :, j2], w_sem.at[5]) for jp in range(2) for j2 in range(2)
    ]
    barrier = pltpu.get_barrier_semaphore()
    for peer in peers:
        pl.semaphore_signal(barrier, inc=1, device_id=peer, device_id_type=MESH)
    for peer in (left, right):
        pl.semaphore_signal(barrier, inc=1, device_id={"tm": peer}, device_id_type=MESH)
    r0, r1 = iota((256, 256), 0), iota((256, 256), 1)
    perm[...] = (r1 == (r0 % 16) * 16 + r0 // 16).astype(F32).astype(BF)
    eye[...] = (r0 == r1).astype(F32).astype(BF)
    avg[...] = jnp.where(iota((16, 256), 0) == iota((16, 256), 1) // 16, 1.0 / PATCH, 0.0).astype(BF)

    g0, f0 = iota((64, 128), 0), iota((64, 128), 1) % 32
    for b in range(4):
        frame = g0 + (32 * b - WINDOW)
        query = f0 + 32 * b
        glob = frame + first
        ok = (jnp.abs(frame - query) <= WINDOW) & (glob >= 0) & (glob < TMS * COUNT)
        ok = ok & ((glob < length) | (frame == query))
        bias[b] = jnp.where(ok, 0.0, -1e30)
    lane_block = iota((64, 128), 1) // 32

    w_copies[1].wait()
    lane = iota((COUNT, COUNT), 1)
    row = iota((COUNT, COUNT), 0)
    negt[...] = jnp.transpose(negs[...].reshape(VIDS * NEG, COUNT).astype(F32))
    ids = negt[pl.ds(pl.multiple_of(PART * vid, PART), PART), :]
    ids = jnp.concatenate([ids] * VIDS, axis=0)
    times = jnp.zeros((COUNT, COUNT), F32)
    for k in range(NEG):
        one = jnp.sum(jnp.where(lane == row // PART * NEG + k, ids, 0.0), axis=1, keepdims=True)
        times += (one * PART + (row % PART).astype(F32) == lane.astype(F32)).astype(F32)
    count_out[...] = times

    pl.semaphore_wait(barrier, VIDS + 2)

    halo_copies = [
        pltpu.make_async_remote_copy(
            src_ref=tokens.at[pl.ds(256 * 7, 256)], dst_ref=halo.at[0],
            send_sem=halo_send.at[0], recv_sem=halo_recv.at[0],
            device_id={"tm": right}, device_id_type=MESH,
        ),
        pltpu.make_async_remote_copy(
            src_ref=tokens.at[pl.ds(0, 256)], dst_ref=halo.at[1],
            send_sem=halo_send.at[1], recv_sem=halo_recv.at[1],
            device_id={"tm": left}, device_id_type=MESH,
        ),
    ]
    for copy in halo_copies:
        copy.start()

    count_copy = pltpu.make_async_remote_copy(
        src_ref=count_out, dst_ref=count, send_sem=c_send, recv_sem=c_recv, device_id=peers[-1], device_id_type=MESH,
    )
    count_copy.start()

    def normed(block, out, rows=(0, 1, 2, 3)):
        for c in rows:
            for n in range(4):
                at = 64 * c + 16 * n
                x = block[at:at + 16, :].astype(F32)
                mean = jnp.sum(x * x, axis=1, keepdims=True) * (1.0 / D)
                out[at:at + 16, :] = (x * lax.rsqrt(mean + 1e-5) * gain[...]).astype(BF)
            yield

    def permuted(y, rows):
        for c in range(4):
            part = nn(perm[...], y[:, 256 * c:256 * c + 256]).astype(BF)
            xn[:, rows, 256 * c:256 * c + 256] = part.reshape(PATCH, 16, 256)
            yield

    def averaged(b):
        tokmean[pl.ds(pl.multiple_of(16 * b, 16), 16), :] = nn(avg[...], raw[b])
        yield

    def rows_of(b):
        return pl.ds(pl.multiple_of(16 * b + 16, 16), 16)

    def flip(a):
        for c in range(4):
            wvt[pl.ds(a, 256), 256 * c:256 * c + 256] = jnp.transpose(wv[256 * c:256 * c + 256, pl.ds(a, 256)])
            yield

    def weave(*jobs):
        for _ in itertools.zip_longest(*jobs):
            pass

    def arrived(b):
        pltpu.make_async_copy(tokens.at[pl.ds(0, 256)], raw.at[b], tok_sem.at[b]).wait()

    arrived(0)
    weave(normed(raw.at[0], y0))
    w_copies[2].start()
    w_copies[0].start()

    def norm_pair(i, carry):
        b = 2 * i
        arrived(b + 1)
        arrived(b + 2)
        weave(permuted(y0, rows_of(b)), normed(raw.at[b + 1], y1), averaged(b))
        weave(permuted(y1, rows_of(b + 1)), normed(raw.at[b + 2], y0), averaged(b + 1))
        return carry

    lax.fori_loop(0, 3, norm_pair, 0)
    arrived(7)
    weave(permuted(y0, rows_of(6)), normed(raw.at[7], y1), averaged(6))
    weave(permuted(y1, rows_of(7)), averaged(7))
    w_copies[3].start()

    w_copies[0].wait()
    w_copies[2].wait()
    scale = math.log2(math.e) / 8.0

    def own_queries(i):
        rows = pl.ds(pl.multiple_of(512 * i, 512), 512)
        x = xn[pl.ds(4 * i, 4), 16:16 + COUNT, :].reshape(512, D)
        for c in range(2):
            queries[rows, 512 * c:512 * c + 512] = (nn(x, wq[:, 512 * c:512 * c + 512]) * scale).astype(BF)
            yield

    def project_queries(i, carry):
        weave(own_queries(i), flip(pl.multiple_of(256 * i, 256)))
        return carry

    lax.fori_loop(0, 4, project_queries, 0)

    for copy in w_copies[4:] + out_copies:
        copy.start()

    def values(ga, ra, gb, rb):
        xa = xn[pl.ds(4 * ga, 4), 32 * ra:32 * ra + 32, :].reshape(128, D)
        xb = xn[pl.ds(4 * gb, 4), 32 * rb:32 * rb + 32, :].reshape(128, D)
        x2 = jnp.concatenate([xa, xb], axis=0)
        for c in range(2):
            r = nt(wvt[512 * c:512 * c + 512], x2).astype(BF)
            vt[ga, 512 * c:512 * c + 512, 128 * ra:128 * ra + 128] = r[:, :128]
            vt[gb, 512 * c:512 * c + 512, 128 * rb:128 * rb + 128] = r[:, 128:]
            yield

    def values_inner(i, carry):
        weave(values(2 * i, 1, 2 * i, 2))
        weave(values(2 * i + 1, 1, 2 * i + 1, 2))
        return carry

    lax.fori_loop(0, 2, values_inner, 0)

    weave(values(0, 3, 1, 3))
    weave(values(2, 3, 3, 3))

    w_copies[3].wait()

    def own_keys(i):
        x = xn[pl.ds(4 * i, 4), 16:16 + COUNT, :].reshape(512, D)
        for c in range(2):
            r = nn(x, wk[:, 512 * c:512 * c + 512]).astype(BF)
            keys[pl.ds(4 * i, 4), 16:16 + COUNT, 512 * c:512 * c + 512] = r.reshape(4, COUNT, 512)
            yield

    def project_keys(i, carry):
        weave(own_keys(i))
        return carry

    lax.fori_loop(0, 3, project_keys, 0)

    halo_copies[0].wait_recv()
    halo_copies[1].wait_recv()
    weave(own_keys(3), normed(halo.at[0], y0), normed(halo.at[1], y1))
    weave(permuted(y0, pl.ds(0, 16)), permuted(y1, pl.ds(16 + COUNT, 16)))
    x = jnp.concatenate([xn[:, :16, :], xn[:, 16 + COUNT:, :]], axis=1).reshape(512, D)
    for c in range(2):
        r = nn(x, wk[:, 512 * c:512 * c + 512]).astype(BF).reshape(PATCH, 32, 512)
        keys[:, :16, 512 * c:512 * c + 512] = r[:, :16]
        keys[:, 16 + COUNT:, 512 * c:512 * c + 512] = r[:, 16:]

    def values_outer(i, carry):
        weave(values(2 * i, 0, 2 * i, 4))
        weave(values(2 * i + 1, 0, 2 * i + 1, 4))
        return carry

    lax.fori_loop(0, 2, values_outer, 0)

    acc[...] = jnp.zeros_like(acc)

    def where_is(u):
        return u // 4, pl.ds(pl.multiple_of(256 * (u % 4), 256), 256)

    head_lanes = [iota((32, 256), 1) // 64 == h for h in range(4)]

    def diagonal(x):
        return [jnp.where(head_lanes[h], x, jnp.zeros_like(x)) for h in range(4)]

    def probs_of(u, out):
        g, cols = where_is(u)
        for q in range(4):
            for b in range(4):
                ps = [8 * g + 2 * q, 8 * g + 2 * q + 1]
                q2 = [queries[pl.ds(pl.multiple_of(COUNT * p + 32 * b, 32), 32), cols] for p in ps]
                k2 = [keys[p, 32 * b:32 * b + 64, cols] for p in ps]
                r = nt(jnp.concatenate(k2, axis=0), jnp.concatenate(diagonal(q2[0]) + diagonal(q2[1]), axis=0))
                for n in range(2):
                    s = r[64 * n:64 * n + 64, 128 * n:128 * n + 128] + bias[b]
                    e = jnp.exp2(s - jnp.max(s, axis=0, keepdims=True))
                    e = (e * (1.0 / jnp.sum(e, axis=0, keepdims=True))).astype(BF)
                    at = 256 * (q // 2) + 64 * (q % 2) + 32 * n
                    out[b, at:at + 32, :] = e[:32]
                    out[b, 128 + at:128 + at + 32, :] = e[32:]
                yield

    def attended_of(u, probs):
        g, rows = where_is(u)
        for b in range(4):
            lanes = slice(128 * b, 128 * b + 256)
            v = jnp.concatenate([vt[2 * g, rows, lanes], vt[2 * g + 1, rows, lanes]], axis=1)
            r = nn(v, probs[b])
            part = r[:64]
            for h in range(1, 4):
                part = jnp.where(lane_block == h, r[64 * h:64 * h + 64], part)
            acc[u % 4, b] += part
            for _ in range(4):
                yield

    weave(probs_of(0, pr0))

    def attend(i, carry):
        u = 2 * i
        weave(probs_of(u + 1, pr1), attended_of(u, pr0))
        weave(probs_of(u + 2, pr0), attended_of(u + 1, pr1))
        return carry

    lax.fori_loop(0, 3, attend, 0)
    def project_out(jp):
        att = []
        for b in range(4):
            pair = jnp.concatenate([acc[2 * jp, b], acc[2 * jp + 1, b]], axis=0)
            turned = jnp.transpose(pair * (1.0 / PATCH)).astype(BF)
            att.append(jnp.concatenate([turned[32 * h:32 * h + 32] for h in range(4)], axis=1))
            yield
        att = jnp.concatenate(att, axis=0)
        for c in range(2):
            tokmean[:, 512 * c:512 * c + 512] += nn(att, wo[jp, :, :, :, 512 * c:512 * c + 512].reshape(512, 512))
            yield

    pltpu.make_async_copy(wo, wo, w_sem.at[5]).wait()
    weave(probs_of(7, pr1), attended_of(6, pr0), project_out(0))
    weave(attended_of(7, pr1))
    weave(project_out(1))

    pooled = tokmean[...]
    blocks = pooled.reshape(VIDS, PART, D)
    pack[...] = jnp.concatenate([blocks[:, :, :HALF], blocks[:, :, HALF:]], axis=1).astype(BF)

    pooled_copies = [
        pltpu.make_async_remote_copy(
            src_ref=pack.at[peers[k]["vid"]], dst_ref=got.at[vid],
            send_sem=a_send, recv_sem=a_recv,
            device_id=peers[k], device_id_type=MESH,
        )
        for k in range(VIDS)
    ]
    near_copies = [
        pltpu.make_async_remote_copy(
            src_ref=pack.at[VIDS - 1], dst_ref=near.at[0],
            send_sem=n_send.at[0], recv_sem=n_recv.at[0],
            device_id={"tm": right}, device_id_type=MESH,
        ),
        pltpu.make_async_remote_copy(
            src_ref=pack.at[0], dst_ref=near.at[1],
            send_sem=n_send.at[1], recv_sem=n_recv.at[1],
            device_id={"tm": left}, device_id_type=MESH,
        ),
    ]
    for copy in pooled_copies + near_copies:
        copy.start()

    w_copies[4].wait()
    own_e[...] = nn(pooled.astype(BF), wp[...]).astype(BF)
    out_copy = pltpu.make_async_copy(own_e, emb_out, out_sem)
    out_copy.start()

    e = own_e[...]
    near_own = nt(e, e)

    def embedded(blocks):
        seen = blocks.astype(F32)
        seen = jnp.concatenate([seen[:, :PART], seen[:, PART:]], axis=2)
        return nn(seen.reshape(-1, D).astype(BF), wp[...]).astype(BF)

    pltpu.make_async_copy(got, got, a_recv).wait()
    all_e = embedded(got[...])
    factor = 8.0 / math.sqrt(E)
    gram = nt(all_e, all_e) * factor

    frame_here = across * COUNT + PART * vid + lane % PART
    other = jnp.zeros((COUNT, COUNT), I32)
    for m in range(VIDS):
        other = jnp.where(lane // PART == m, valid[m], other)
    count_copy.wait_recv()
    times = count[...]
    neg = jnp.where(frame_here < other, gram, -1e30)
    top = jnp.max(jnp.where(times > 0, neg, -3e38), axis=1, keepdims=True)
    some = jnp.sum(jnp.where(times > 0, times * jnp.exp(jnp.minimum(neg - top, 0.0)), 0.0), axis=1, keepdims=True)
    lse = top + jnp.log(some)
    lse_out[...] = jnp.broadcast_to(lse, (COUNT, 128)).reshape(VIDS, PART, 128)

    back_copies = [
        pltpu.make_async_remote_copy(
            src_ref=lse_out.at[peers[k]["vid"]], dst_ref=lse_in.at[vid],
            send_sem=b_send, recv_sem=b_recv,
            device_id=peers[k], device_id_type=MESH,
        )
        for k in range(VIDS)
    ]
    for copy in back_copies:
        copy.start()

    for copy in near_copies:
        copy.wait_recv()
    near_e = nt(embedded(near[...]), e)
    scores = jnp.concatenate([near_e[:REACH], near_own, near_e[REACH:]], axis=0)
    off = offsets[...]
    here = first + iota((1, COUNT), 1)
    ahead = here + off
    inside = (ahead >= 0) & (ahead < length)
    slot = jnp.where(inside, ahead, here - off) - first + REACH
    pick = iota((COUNT + 2 * REACH, COUNT), 0) == slot
    pos = jnp.sum(jnp.where(pick, scores, 0.0), axis=0, keepdims=True) * factor

    pltpu.make_async_copy(lse_in, lse_in, b_recv).wait()
    back = lse_in[...].reshape(COUNT, 128)
    lse_neg = jnp.sum(jnp.where(row == lane, back, 0.0), axis=0, keepdims=True)
    peak = jnp.maximum(pos, lse_neg)
    total = peak + jnp.log(jnp.exp(pos - peak) + jnp.exp(lse_neg - peak))
    loss_out[...] = jnp.where(here < length, total - pos, 0.0)

    for copy in halo_copies + near_copies + [count_copy]:
        copy.wait_send()
    pltpu.make_async_copy(pack, pack, a_send).wait()
    pltpu.make_async_copy(lse_out, lse_out, b_send).wait()
    out_copy.wait()


def hand_over(emb, losses, emb_out, loss_out):
    emb_out[...] = emb[...]
    loss_out[...] = losses[...]


def local(tokens, norm_gain, w_qkv, w_out, w_proj, offsets, negatives, valid):
    anywhere = pl.BlockSpec(memory_space=pl.ANY)
    vmem = pl.BlockSpec(memory_space=pltpu.VMEM)
    dma = pltpu.SemaphoreType.DMA
    emb, losses = pl.pallas_call(
        kernel,
        out_shape=(
            jax.ShapeDtypeStruct((COUNT, E), BF),
            jax.ShapeDtypeStruct((1, COUNT), F32),
        ),
        in_specs=[
            pl.BlockSpec(memory_space=pltpu.SMEM), anywhere, vmem, anywhere, anywhere, anywhere, vmem, anywhere,
        ],
        out_specs=(anywhere, vmem),
        scratch_shapes=[
            pltpu.VMEM((256, 256), BF),
            pltpu.VMEM((256, 256), BF),
            pltpu.VMEM((16, 256), BF),
            pltpu.VMEM((8, 256, D), BF),
            pltpu.VMEM((2, 256, D), BF),
            pltpu.VMEM((D, D), BF),
            pltpu.VMEM((D, D), BF),
            pltpu.VMEM((D, D), BF),
            pltpu.VMEM((2, 4, 2, 64, D), BF),
            pltpu.VMEM((D, E), BF),
            pltpu.VMEM((VIDS, NEG, COUNT), I32),
            pltpu.VMEM((COUNT, VIDS * NEG), F32),
            pltpu.VMEM((D, D), BF),
            pltpu.VMEM((PATCH, 160, D), BF),
            pltpu.VMEM((PATCH, 160, D), BF),
            pltpu.VMEM((PATCH * COUNT, D), BF),
            pltpu.VMEM((4, D, 640), BF),
            pltpu.VMEM((256, D), BF),
            pltpu.VMEM((256, D), BF),
            pltpu.VMEM((4, 64, 128), F32),
            pltpu.VMEM((4, 4, 64, 256), F32),
            pltpu.VMEM((4, 4, 64, 256), F32),
            pltpu.VMEM((4, 512, 128), BF),
            pltpu.VMEM((4, 512, 128), BF),
            pltpu.VMEM((COUNT, D), F32),
            pltpu.VMEM((4, 4, 64, 128), F32),
            pltpu.VMEM((VIDS, 16, HALF), BF),
            pltpu.VMEM((VIDS, 16, HALF), BF),
            pltpu.VMEM((2, 16, HALF), BF),
            pltpu.VMEM((COUNT, E), BF),
            pltpu.VMEM((COUNT, COUNT), F32),
            pltpu.VMEM((COUNT, COUNT), F32),
            pltpu.VMEM((VIDS, PART, 128), F32),
            pltpu.VMEM((VIDS, PART, 128), F32),
            dma((8,)), dma((6,)), dma, dma((2,)), dma((2,)), dma, dma, dma((2,)), dma((2,)), dma, dma, dma, dma,
        ],
        compiler_params=pltpu.CompilerParams(
            collective_id=0, has_side_effects=True, vmem_limit_bytes=60 * 1024 * 1024
        ),
    )(
        valid,
        tokens.reshape(COUNT * PATCH, D),
        norm_gain.reshape(1, D),
        w_qkv,
        w_out.reshape(2, 2, 4, 64, D),
        w_proj,
        offsets,
        jnp.swapaxes(negatives, 1, 2),
    )
    emb, losses = pl.pallas_call(
        hand_over,
        out_shape=(
            jax.ShapeDtypeStruct((COUNT, E), BF),
            jax.ShapeDtypeStruct((1, COUNT), F32),
        ),
        in_specs=[vmem, vmem],
        out_specs=(vmem, vmem),
    )(emb, losses)
    return emb.reshape(1, COUNT, E), losses


def solution(mesh):
    placed = (
        P("vid", "tm", None, None),
        P(),
        P(),
        P(),
        P(),
        P("vid", "tm"),
        P(None, "tm", None),
        P(),
    )
    return jax.shard_map(
        local,
        mesh=mesh,
        in_specs=placed,
        out_specs=(P("vid", "tm", None), P("vid", "tm")),
        check_vma=False,
    )
```

```python
import itertools
import math

import jax
import jax.numpy as jnp
from jax import lax
from jax.experimental import pallas as pl
from jax.experimental.pallas import tpu as pltpu
from jax.sharding import PartitionSpec as P

MESH = pl.DeviceIdType.MESH
BF, F32, I32 = jnp.bfloat16, jnp.float32, jnp.int32
D = 1024
E = 2048
PATCH = 16
WINDOW = 16
REACH = 8
COUNT = 128
VIDS = 16
TMS = 8
NEG = 8
PART = COUNT // VIDS
HALF = D // 2


def nn(a, b):
    return lax.dot_general(a, b, (((1,), (0,)), ((), ())), preferred_element_type=F32)


def nt(a, b):
    return lax.dot_general(a, b, (((1,), (1,)), ((), ())), preferred_element_type=F32)


def iota(shape, dim):
    return lax.broadcasted_iota(I32, shape, dim)


def kernel(
    valid, tokens, gain, w_qkv, w_out, w_proj, offsets, negatives,
    emb_out, loss_out,
    perm, eye, avg, raw, halo, wq, wk, wv, wo, wp, negs, negt, wvt, xn, keys, queries, vt, y0, y1,
    bias, st0, st1, pr0, pr1, tokmean, acc, pack, got, near, own_e, count_out, count, lse_out, lse_in,
    tok_sem, w_sem, out_sem, halo_send, halo_recv, a_send, a_recv, n_send, n_recv, b_send, b_recv, c_send, c_recv,
):
    vid = lax.axis_index("vid")
    tm = lax.axis_index("tm")
    left = lax.rem(tm + TMS - 1, TMS)
    right = lax.rem(tm + 1, TMS)
    across = lax.rem(tm + TMS // 2, TMS)
    y_hi, z, core = vid // 8, vid // 2 % 4, vid % 2
    peers = [
        {"vid": (y_hi + dy) % 2 * 8 + (z + dz) % 4 * 2 + (core + dc) % 2, "tm": across}
        for dz in (2, 1, 3, 0) for dy in (1, 0) for dc in (1, 0)
    ]
    first = tm * COUNT
    length = valid[vid]

    tok_copies = [
        pltpu.make_async_copy(tokens.at[pl.ds(256 * b, 256)], raw.at[b], tok_sem.at[b])
        for b in range(8)
    ]
    w_copies = [
        pltpu.make_async_copy(src, dst, w_sem.at[i])
        for i, (src, dst) in enumerate(
            [
                (w_qkv.at[:, pl.ds(2 * D, D)], wv),
                (negatives, negs),
                (w_qkv.at[:, pl.ds(0, D)], wq),
                (w_qkv.at[:, pl.ds(D, D)], wk),
                (w_proj, wp),
            ]
        )
    ]
    w_copies[1].start()
    tok_copies[0].start()
    for copy in tok_copies[1:]:
        copy.start()
    out_copies = [
        pltpu.make_async_copy(w_out.at[jp, j2], wo.at[jp, :, j2], w_sem.at[5]) for jp in range(2) for j2 in range(2)
    ]
    barrier = pltpu.get_barrier_semaphore()
    for peer in peers:
        pl.semaphore_signal(barrier, inc=1, device_id=peer, device_id_type=MESH)
    for peer in (left, right):
        pl.semaphore_signal(barrier, inc=1, device_id={"tm": peer}, device_id_type=MESH)
    r0, r1 = iota((256, 256), 0), iota((256, 256), 1)
    perm[...] = (r1 == (r0 % 16) * 16 + r0 // 16).astype(F32).astype(BF)
    eye[...] = (r0 == r1).astype(F32).astype(BF)
    avg[...] = jnp.where(iota((16, 256), 0) == iota((16, 256), 1) // 16, 1.0 / PATCH, 0.0).astype(BF)

    g0, f0 = iota((64, 128), 0), iota((64, 128), 1) % 32
    for b in range(4):
        frame = g0 + (32 * b - WINDOW)
        query = f0 + 32 * b
        glob = frame + first
        ok = (jnp.abs(frame - query) <= WINDOW) & (glob >= 0) & (glob < TMS * COUNT)
        ok = ok & ((glob < length) | (frame == query))
        bias[b] = jnp.where(ok, 0.0, -1e30)
    lane_block = iota((64, 128), 1) // 32

    pl.semaphore_wait(barrier, VIDS + 2)

    halo_copies = [
        pltpu.make_async_remote_copy(
            src_ref=tokens.at[pl.ds(256 * 7, 256)], dst_ref=halo.at[0],
            send_sem=halo_send.at[0], recv_sem=halo_recv.at[0],
            device_id={"tm": right}, device_id_type=MESH,
        ),
        pltpu.make_async_remote_copy(
            src_ref=tokens.at[pl.ds(0, 256)], dst_ref=halo.at[1],
            send_sem=halo_send.at[1], recv_sem=halo_recv.at[1],
            device_id={"tm": left}, device_id_type=MESH,
        ),
    ]
    for copy in halo_copies:
        copy.start()

    def normed(block, out, rows=(0, 1, 2, 3)):
        for c in rows:
            for n in range(4):
                at = 64 * c + 16 * n
                x = block[at:at + 16, :].astype(F32)
                mean = jnp.sum(x * x, axis=1, keepdims=True) * (1.0 / D)
                out[at:at + 16, :] = (x * lax.rsqrt(mean + 1e-5) * gain[...]).astype(BF)
            yield

    def permuted(y, rows):
        for c in range(4):
            part = nn(perm[...], y[:, 256 * c:256 * c + 256]).astype(BF)
            xn[:, rows, 256 * c:256 * c + 256] = part.reshape(PATCH, 16, 256)
            yield

    def averaged(b):
        tokmean[pl.ds(pl.multiple_of(16 * b, 16), 16), :] = nn(avg[...], raw[b])
        yield

    def rows_of(b):
        return pl.ds(pl.multiple_of(16 * b + 16, 16), 16)

    def flip(a):
        for c in range(4):
            wvt[pl.ds(a, 256), 256 * c:256 * c + 256] = jnp.transpose(wv[256 * c:256 * c + 256, pl.ds(a, 256)])
            yield

    def weave(*jobs):
        for _ in itertools.zip_longest(*jobs):
            pass

    def arrived(b):
        pltpu.make_async_copy(tokens.at[pl.ds(0, 256)], raw.at[b], tok_sem.at[b]).wait()

    arrived(0)
    weave(normed(raw.at[0], y0))
    w_copies[2].start()
    w_copies[0].start()

    def norm_pair(i, carry):
        b = 2 * i
        arrived(b + 1)
        arrived(b + 2)
        weave(permuted(y0, rows_of(b)), normed(raw.at[b + 1], y1), averaged(b))
        weave(permuted(y1, rows_of(b + 1)), normed(raw.at[b + 2], y0), averaged(b + 1))
        return carry

    lax.fori_loop(0, 3, norm_pair, 0)
    arrived(7)
    weave(permuted(y0, rows_of(6)), normed(raw.at[7], y1), averaged(6))
    weave(permuted(y1, rows_of(7)), averaged(7))
    w_copies[3].start()

    w_copies[0].wait()
    w_copies[2].wait()
    scale = math.log2(math.e) / 8.0

    def own_queries(i):
        rows = pl.ds(pl.multiple_of(512 * i, 512), 512)
        x = xn[pl.ds(4 * i, 4), 16:16 + COUNT, :].reshape(512, D)
        for c in range(2):
            queries[rows, 512 * c:512 * c + 512] = (nn(x, wq[:, 512 * c:512 * c + 512]) * scale).astype(BF)
            yield

    def project_queries(i, carry):
        weave(own_queries(i), flip(pl.multiple_of(256 * i, 256)))
        return carry

    lax.fori_loop(0, 4, project_queries, 0)

    for copy in w_copies[4:] + out_copies:
        copy.start()

    def values(ga, ra, gb, rb):
        xa = xn[pl.ds(4 * ga, 4), 32 * ra:32 * ra + 32, :].reshape(128, D)
        xb = xn[pl.ds(4 * gb, 4), 32 * rb:32 * rb + 32, :].reshape(128, D)
        x2 = jnp.concatenate([xa, xb], axis=0)
        for c in range(2):
            r = nt(wvt[512 * c:512 * c + 512], x2).astype(BF)
            vt[ga, 512 * c:512 * c + 512, 128 * ra:128 * ra + 128] = r[:, :128]
            vt[gb, 512 * c:512 * c + 512, 128 * rb:128 * rb + 128] = r[:, 128:]
            yield

    def values_inner(i, carry):
        weave(values(2 * i, 1, 2 * i, 2))
        weave(values(2 * i + 1, 1, 2 * i + 1, 2))
        return carry

    w_copies[1].wait()
    lax.fori_loop(0, 2, values_inner, 0)

    lane = iota((COUNT, COUNT), 1)
    row = iota((COUNT, COUNT), 0)
    negt[...] = jnp.transpose(negs[...].reshape(VIDS * NEG, COUNT).astype(F32))
    ids = negt[pl.ds(pl.multiple_of(PART * vid, PART), PART), :]
    ids = jnp.concatenate([ids] * VIDS, axis=0)
    times = jnp.zeros((COUNT, COUNT), F32)
    for k in range(NEG):
        one = jnp.sum(jnp.where(lane == row // PART * NEG + k, ids, 0.0), axis=1, keepdims=True)
        times += (one * PART + (row % PART).astype(F32) == lane.astype(F32)).astype(F32)
    count_out[...] = times
    weave(values(0, 3, 1, 3))
    weave(values(2, 3, 3, 3))
    count_copy = pltpu.make_async_remote_copy(
        src_ref=count_out, dst_ref=count, send_sem=c_send, recv_sem=c_recv, device_id=peers[-1], device_id_type=MESH,
    )
    count_copy.start()

    w_copies[3].wait()

    def own_keys(i):
        x = xn[pl.ds(4 * i, 4), 16:16 + COUNT, :].reshape(512, D)
        for c in range(2):
            r = nn(x, wk[:, 512 * c:512 * c + 512]).astype(BF)
            keys[pl.ds(4 * i, 4), 16:16 + COUNT, 512 * c:512 * c + 512] = r.reshape(4, COUNT, 512)
            yield

    def project_keys(i, carry):
        weave(own_keys(i))
        return carry

    lax.fori_loop(0, 3, project_keys, 0)

    halo_copies[0].wait_recv()
    halo_copies[1].wait_recv()
    weave(own_keys(3), normed(halo.at[0], y0), normed(halo.at[1], y1))
    weave(permuted(y0, pl.ds(0, 16)), permuted(y1, pl.ds(16 + COUNT, 16)))
    x = jnp.concatenate([xn[:, :16, :], xn[:, 16 + COUNT:, :]], axis=1).reshape(512, D)
    for c in range(2):
        r = nn(x, wk[:, 512 * c:512 * c + 512]).astype(BF).reshape(PATCH, 32, 512)
        keys[:, :16, 512 * c:512 * c + 512] = r[:, :16]
        keys[:, 16 + COUNT:, 512 * c:512 * c + 512] = r[:, 16:]

    def values_outer(i, carry):
        weave(values(2 * i, 0, 2 * i, 4))
        weave(values(2 * i + 1, 0, 2 * i + 1, 4))
        return carry

    lax.fori_loop(0, 2, values_outer, 0)

    acc[...] = jnp.zeros_like(acc)

    def where_is(u):
        return u // 4, pl.ds(pl.multiple_of(256 * (u % 4), 256), 256)

    head_lanes = [iota((32, 256), 1) // 64 == h for h in range(4)]

    def diagonal(x):
        return [jnp.where(head_lanes[h], x, jnp.zeros_like(x)) for h in range(4)]

    def probs_of(u, out):
        g, cols = where_is(u)
        for q in range(4):
            for b in range(4):
                ps = [8 * g + 2 * q, 8 * g + 2 * q + 1]
                q2 = [queries[pl.ds(pl.multiple_of(COUNT * p + 32 * b, 32), 32), cols] for p in ps]
                k2 = [keys[p, 32 * b:32 * b + 64, cols] for p in ps]
                r = nt(jnp.concatenate(k2, axis=0), jnp.concatenate(diagonal(q2[0]) + diagonal(q2[1]), axis=0))
                for n in range(2):
                    s = r[64 * n:64 * n + 64, 128 * n:128 * n + 128] + bias[b]
                    e = jnp.exp2(s - jnp.max(s, axis=0, keepdims=True))
                    e = (e * (1.0 / jnp.sum(e, axis=0, keepdims=True))).astype(BF)
                    at = 256 * (q // 2) + 64 * (q % 2) + 32 * n
                    out[b, at:at + 32, :] = e[:32]
                    out[b, 128 + at:128 + at + 32, :] = e[32:]
                yield

    def attended_of(u, probs):
        g, rows = where_is(u)
        for b in range(4):
            lanes = slice(128 * b, 128 * b + 256)
            v = jnp.concatenate([vt[2 * g, rows, lanes], vt[2 * g + 1, rows, lanes]], axis=1)
            r = nn(v, probs[b])
            part = r[:64]
            for h in range(1, 4):
                part = jnp.where(lane_block == h, r[64 * h:64 * h + 64], part)
            acc[u % 4, b] += part
            for _ in range(4):
                yield

    weave(probs_of(0, pr0))

    def attend(i, carry):
        u = 2 * i
        weave(probs_of(u + 1, pr1), attended_of(u, pr0))
        weave(probs_of(u + 2, pr0), attended_of(u + 1, pr1))
        return carry

    lax.fori_loop(0, 3, attend, 0)
    def project_out(jp):
        att = []
        for b in range(4):
            pair = jnp.concatenate([acc[2 * jp, b], acc[2 * jp + 1, b]], axis=0)
            turned = jnp.transpose(pair * (1.0 / PATCH)).astype(BF)
            att.append(jnp.concatenate([turned[32 * h:32 * h + 32] for h in range(4)], axis=1))
            yield
        att = jnp.concatenate(att, axis=0)
        for c in range(2):
            tokmean[:, 512 * c:512 * c + 512] += nn(att, wo[jp, :, :, :, 512 * c:512 * c + 512].reshape(512, 512))
            yield

    pltpu.make_async_copy(wo, wo, w_sem.at[5]).wait()
    weave(probs_of(7, pr1), attended_of(6, pr0), project_out(0))
    weave(attended_of(7, pr1))
    weave(project_out(1))

    pooled = tokmean[...]
    blocks = pooled.reshape(VIDS, PART, D)
    pack[...] = jnp.concatenate([blocks[:, :, :HALF], blocks[:, :, HALF:]], axis=1).astype(BF)

    pooled_copies = [
        pltpu.make_async_remote_copy(
            src_ref=pack.at[peers[k]["vid"]], dst_ref=got.at[vid],
            send_sem=a_send, recv_sem=a_recv,
            device_id=peers[k], device_id_type=MESH,
        )
        for k in range(VIDS)
    ]
    near_copies = [
        pltpu.make_async_remote_copy(
            src_ref=pack.at[VIDS - 1], dst_ref=near.at[0],
            send_sem=n_send.at[0], recv_sem=n_recv.at[0],
            device_id={"tm": right}, device_id_type=MESH,
        ),
        pltpu.make_async_remote_copy(
            src_ref=pack.at[0], dst_ref=near.at[1],
            send_sem=n_send.at[1], recv_sem=n_recv.at[1],
            device_id={"tm": left}, device_id_type=MESH,
        ),
    ]
    for copy in pooled_copies + near_copies:
        copy.start()

    w_copies[4].wait()
    own_e[...] = nn(pooled.astype(BF), wp[...]).astype(BF)
    out_copy = pltpu.make_async_copy(own_e, emb_out, out_sem)
    out_copy.start()

    e = own_e[...]
    near_own = nt(e, e)

    def embedded(blocks):
        seen = blocks.astype(F32)
        seen = jnp.concatenate([seen[:, :PART], seen[:, PART:]], axis=2)
        return nn(seen.reshape(-1, D).astype(BF), wp[...]).astype(BF)

    pltpu.make_async_copy(got, got, a_recv).wait()
    all_e = embedded(got[...])
    factor = 8.0 / math.sqrt(E)
    gram = nt(all_e, all_e) * factor

    frame_here = across * COUNT + PART * vid + lane % PART
    other = jnp.zeros((COUNT, COUNT), I32)
    for m in range(VIDS):
        other = jnp.where(lane // PART == m, valid[m], other)
    count_copy.wait_recv()
    times = count[...]
    neg = jnp.where(frame_here < other, gram, -1e30)
    top = jnp.max(jnp.where(times > 0, neg, -3e38), axis=1, keepdims=True)
    some = jnp.sum(jnp.where(times > 0, times * jnp.exp(jnp.minimum(neg - top, 0.0)), 0.0), axis=1, keepdims=True)
    lse = top + jnp.log(some)
    lse_out[...] = jnp.broadcast_to(lse, (COUNT, 128)).reshape(VIDS, PART, 128)

    back_copies = [
        pltpu.make_async_remote_copy(
            src_ref=lse_out.at[peers[k]["vid"]], dst_ref=lse_in.at[vid],
            send_sem=b_send, recv_sem=b_recv,
            device_id=peers[k], device_id_type=MESH,
        )
        for k in range(VIDS)
    ]
    for copy in back_copies:
        copy.start()

    for copy in near_copies:
        copy.wait_recv()
    near_e = nt(embedded(near[...]), e)
    scores = jnp.concatenate([near_e[:REACH], near_own, near_e[REACH:]], axis=0)
    off = offsets[...]
    here = first + iota((1, COUNT), 1)
    ahead = here + off
    inside = (ahead >= 0) & (ahead < length)
    slot = jnp.where(inside, ahead, here - off) - first + REACH
    pick = iota((COUNT + 2 * REACH, COUNT), 0) == slot
    pos = jnp.sum(jnp.where(pick, scores, 0.0), axis=0, keepdims=True) * factor

    pltpu.make_async_copy(lse_in, lse_in, b_recv).wait()
    back = lse_in[...].reshape(COUNT, 128)
    lse_neg = jnp.sum(jnp.where(row == lane, back, 0.0), axis=0, keepdims=True)
    peak = jnp.maximum(pos, lse_neg)
    total = peak + jnp.log(jnp.exp(pos - peak) + jnp.exp(lse_neg - peak))
    loss_out[...] = jnp.where(here < length, total - pos, 0.0)

    for copy in halo_copies + near_copies + [count_copy]:
        copy.wait_send()
    pltpu.make_async_copy(pack, pack, a_send).wait()
    pltpu.make_async_copy(lse_out, lse_out, b_send).wait()
    out_copy.wait()


def hand_over(emb, losses, emb_out, loss_out):
    emb_out[...] = emb[...]
    loss_out[...] = losses[...]


def local(tokens, norm_gain, w_qkv, w_out, w_proj, offsets, negatives, valid):
    anywhere = pl.BlockSpec(memory_space=pl.ANY)
    vmem = pl.BlockSpec(memory_space=pltpu.VMEM)
    dma = pltpu.SemaphoreType.DMA
    emb, losses = pl.pallas_call(
        kernel,
        out_shape=(
            jax.ShapeDtypeStruct((COUNT, E), BF),
            jax.ShapeDtypeStruct((1, COUNT), F32),
        ),
        in_specs=[
            pl.BlockSpec(memory_space=pltpu.SMEM), anywhere, vmem, anywhere, anywhere, anywhere, vmem, anywhere,
        ],
        out_specs=(anywhere, vmem),
        scratch_shapes=[
            pltpu.VMEM((256, 256), BF),
            pltpu.VMEM((256, 256), BF),
            pltpu.VMEM((16, 256), BF),
            pltpu.VMEM((8, 256, D), BF),
            pltpu.VMEM((2, 256, D), BF),
            pltpu.VMEM((D, D), BF),
            pltpu.VMEM((D, D), BF),
            pltpu.VMEM((D, D), BF),
            pltpu.VMEM((2, 4, 2, 64, D), BF),
            pltpu.VMEM((D, E), BF),
            pltpu.VMEM((VIDS, NEG, COUNT), I32),
            pltpu.VMEM((COUNT, VIDS * NEG), F32),
            pltpu.VMEM((D, D), BF),
            pltpu.VMEM((PATCH, 160, D), BF),
            pltpu.VMEM((PATCH, 160, D), BF),
            pltpu.VMEM((PATCH * COUNT, D), BF),
            pltpu.VMEM((4, D, 640), BF),
            pltpu.VMEM((256, D), BF),
            pltpu.VMEM((256, D), BF),
            pltpu.VMEM((4, 64, 128), F32),
            pltpu.VMEM((4, 4, 64, 256), F32),
            pltpu.VMEM((4, 4, 64, 256), F32),
            pltpu.VMEM((4, 512, 128), BF),
            pltpu.VMEM((4, 512, 128), BF),
            pltpu.VMEM((COUNT, D), F32),
            pltpu.VMEM((4, 4, 64, 128), F32),
            pltpu.VMEM((VIDS, 16, HALF), BF),
            pltpu.VMEM((VIDS, 16, HALF), BF),
            pltpu.VMEM((2, 16, HALF), BF),
            pltpu.VMEM((COUNT, E), BF),
            pltpu.VMEM((COUNT, COUNT), F32),
            pltpu.VMEM((COUNT, COUNT), F32),
            pltpu.VMEM((VIDS, PART, 128), F32),
            pltpu.VMEM((VIDS, PART, 128), F32),
            dma((8,)), dma((6,)), dma, dma((2,)), dma((2,)), dma, dma, dma((2,)), dma((2,)), dma, dma, dma, dma,
        ],
        compiler_params=pltpu.CompilerParams(
            collective_id=0, has_side_effects=True, vmem_limit_bytes=60 * 1024 * 1024
        ),
    )(
        valid,
        tokens.reshape(COUNT * PATCH, D),
        norm_gain.reshape(1, D),
        w_qkv,
        w_out.reshape(2, 2, 4, 64, D),
        w_proj,
        offsets,
        jnp.swapaxes(negatives, 1, 2),
    )
    emb, losses = pl.pallas_call(
        hand_over,
        out_shape=(
            jax.ShapeDtypeStruct((COUNT, E), BF),
            jax.ShapeDtypeStruct((1, COUNT), F32),
        ),
        in_specs=[vmem, vmem],
        out_specs=(vmem, vmem),
    )(emb, losses)
    return emb.reshape(1, COUNT, E), losses


def solution(mesh):
    placed = (
        P("vid", "tm", None, None),
        P(),
        P(),
        P(),
        P(),
        P("vid", "tm"),
        P(None, "tm", None),
        P(),
    )
    return jax.shard_map(
        local,
        mesh=mesh,
        in_specs=placed,
        out_specs=(P("vid", "tm", None), P("vid", "tm")),
        check_vma=False,
    )
```
